32 devices in a mesh: grp: 4 (over y, core), pair: 8 (over z, x).
Axes of the slice: x: 2, y: 2, z: 4, core: 2. Of those that a mesh axis runs over, the one named last changes fastest.
Arguments:
- amplitudes: bfloat16 [4, 32, 1024, 1024], P('grp', 'pair'), may hold values from -6 to 6
- vv_fock: bfloat16 [1024, 1024], replicated, may hold values from -0.1875 to 0.1875
- cycle_panels: bfloat16 [2, 1024, 2048], P(None, 'pair', 'grp'), may hold values from -0.125 to 0.125
- row_energy: float32 [2], replicated, may hold values from -2 to -0.5
- col_energy: float32 [64], P('grp'), may hold values from -2 to -0.5
- virt_energy: float32 [1024], replicated, may hold values from 0.2 to 3
Outputs:
- new_amplitudes: bfloat16 [4, 32, 1024, 1024], P('grp', 'pair')
The draws below stay inside these ranges and needn't reach their ends.
All inputs are finite; a program needn't handle non-finite values.
Results may differ from the reference program's by a relative error of at most 0.0049.
Values may be sent and summed in bfloat16 or wider, within the bound.
No kernel may reach another device: no remote copies, remote signals or barrier semaphores. Data moves between devices by JAX's collectives and lax.ppermute only.
A program may use at most 128 MiB of HBM per device.

```python
import jax
import jax.numpy as jnp
from jax import lax

V = 1024
NO = 2
JG = 16
NJ = 64
N_GRP = 4


def levels(rng, extent, cuts, low, high):
    def one(position, blocks):
        steps = jax.random.uniform(jax.random.fold_in(jax.random.fold_in(rng, 6), position), (blocks,), jnp.float32, low / len(cuts), high / len(cuts))
        return jnp.repeat(jnp.exp(steps), extent[position] // blocks).reshape((-1,) + (1,) * (len(extent) - position - 1))

    level = one(*cuts[0])
    for cut in cuts[1:]:
        level = level * one(*cut)
    return level


def normal_values(stream_key, shape, scale, bound, cuts=(), dtype=jnp.bfloat16):
    result = scale * jax.random.normal(stream_key, shape, jnp.float32)
    if cuts:
        result = result * levels(stream_key, shape, cuts, -0.22, 0.18)
    return jnp.clip(result, -bound, bound).astype(dtype)


def setup_inputs(seed: int = 0) -> dict:
    key_list = jax.random.split(jax.random.key(seed), 7)
    return {
        "amplitudes": normal_values(key_list[0], (N_GRP, NO * JG, V, V), 1.0, 6.0, ((0, 4), (1, 8))),
        "vv_fock": normal_values(key_list[1], (V, V), V ** -0.5, 0.1875),
        "cycle_panels": normal_values(key_list[2], (NO, V, NO * V), (NO * V) ** -0.5, 0.125, ((1, 8), (2, 4))),
        "row_energy": jnp.clip(jax.random.uniform(key_list[3], (NO,), jnp.float32, -2.0, -0.5), -2.0, -0.5),
        "col_energy": jnp.clip(-2.0 + 1.5 * jax.random.uniform(key_list[4], (NJ,), jnp.float32) ** levels(key_list[4], (NJ,), ((0, 4),), -0.2, 0.2), -2.0, -0.5),
        "virt_energy": jnp.clip(jax.random.uniform(key_list[5], (V,), jnp.float32, 0.2, 3.0), 0.2, 3.0),
    }


def reference(amplitudes, vv_fock, cycle_panels, row_energy, col_energy, virt_energy):
    fock_matrix = vv_fock.astype(jnp.float32)
    panels = cycle_panels.astype(jnp.float32).reshape(NO, V, NO, V)

    def one_group(inputs):
        group_amps, group_energy = inputs
        amps_wide = group_amps.astype(jnp.float32)
        dressed = (jnp.einsum('ac,pcb->pab', fock_matrix, amps_wide, precision=lax.Precision.HIGHEST)
                   + jnp.einsum('pac,bc->pab', amps_wide, fock_matrix, precision=lax.Precision.HIGHEST)).astype(jnp.bfloat16)
        column = dressed.astype(jnp.float32).reshape(NO, JG, V, V)
        cycle_term = jnp.einsum('ibkc,kjac->ijab', panels, column, precision=lax.Precision.HIGHEST)
        divisor = ((virt_energy[None, None, :, None] + virt_energy[None, None, None, :])
                   - row_energy[:, None, None, None]) - group_energy[None, :, None, None]
        return ((column + cycle_term) / divisor).astype(jnp.bfloat16).reshape(NO * JG, V, V)

    return lax.map(one_group, (amplitudes, col_energy.reshape(N_GRP, JG)))
```

```python
import jax
import jax.numpy as jnp
from jax import lax
from jax.sharding import Mesh, PartitionSpec as P

ROWS = 256
SWAP = [(0, 1), (1, 0)]


def shards(amplitudes, vv_fock, cycle_panels, row_energy, col_energy, virt_energy):
    amps = amplitudes[0]
    per_dev, virt_count, _ = amps.shape
    group_j = col_energy.shape[0]
    half = lax.axis_index("half")
    rest = lax.axis_index("rest")
    rows = min(ROWS, virt_count)

    kept = lax.dynamic_index_in_dim(cycle_panels, half, 0, keepdims=False)
    given = lax.dynamic_index_in_dim(cycle_panels, 1 - half, 0, keepdims=False)
    got = lax.ppermute(given, "half", SWAP)

    chunks = [(p, a) for p in range(per_dev) for a in range(0, virt_count, rows)]
    own, other = [], []
    for p, a in chunks:
        piece = (
            jnp.dot(vv_fock[a : a + rows], amps[p], preferred_element_type=jnp.float32)
            + lax.dot_general(
                amps[p, a : a + rows], vv_fock, (((1,), (1,)), ((), ())), preferred_element_type=jnp.float32
            )
        ).astype(jnp.bfloat16)
        own.append(piece)
        other.append(lax.ppermute(piece, "half", SWAP))

    first = jnp.where(half == 0, kept, got)
    second = jnp.where(half == 0, got, kept)
    panel = lax.all_gather(jnp.stack([first, second]), "grp", axis=2, tiled=True)
    panel = lax.all_gather(panel, "rest", axis=1, tiled=True)
    panel = panel.reshape(virt_count, 2, virt_count)
    own_panel = lax.dynamic_index_in_dim(panel, half, 1, keepdims=False)
    other_panel = lax.dynamic_index_in_dim(panel, 1 - half, 1, keepdims=False)

    row = lax.dynamic_index_in_dim(row_energy, half, 0, keepdims=False)
    out = jnp.zeros(amps.shape, jnp.bfloat16)
    for (p, a), mine, theirs in zip(chunks, own, other):
        nt = (((1,), (1,)), ((), ()))
        total = (
            mine.astype(jnp.float32)
            + lax.dot_general(mine, own_panel, nt, preferred_element_type=jnp.float32)
            + lax.dot_general(theirs, other_panel, nt, preferred_element_type=jnp.float32)
        )
        col = lax.dynamic_index_in_dim(col_energy, (rest * per_dev + p) % group_j, 0, keepdims=False)
        divisor = ((virt_energy[a : a + rows, None] + virt_energy[None, :]) - row) - col
        out = lax.dynamic_update_slice(out, (total / divisor).astype(jnp.bfloat16)[None], (p, a, 0))
    return out[None]


def solution(mesh):
    n_grp, n_pair = mesh.shape["grp"], mesh.shape["pair"]
    split = Mesh(mesh.devices.reshape(n_grp, 2, n_pair // 2), ("grp", "half", "rest"))
    pair = ("half", "rest")
    in_specs = (P("grp", pair, None, None), P(), P(None, pair, "grp"), P(), P("grp"), P())
    out_specs = P("grp", pair, None, None)
    return jax.shard_map(shards, mesh=split, in_specs=in_specs, out_specs=out_specs, check_vma=False)
```

```python
import jax
import jax.numpy as jnp
from jax import lax
from jax.sharding import Mesh, PartitionSpec as P

ROWS = 256
DEPTH = 3
SWAP = [(0, 1), (1, 0)]
NT = (((1,), (1,)), ((), ()))


def after(value, event):
    return lax.optimization_barrier((value, event))[0]


def shards(amplitudes, vv_fock, cycle_panels, row_energy, col_energy, virt_energy):
    amps = amplitudes[0]
    per_dev, virt_count, _ = amps.shape
    group_j = col_energy.shape[0]
    n_grp, n_rest = lax.axis_size("grp"), lax.axis_size("rest")
    half, rest = (lax.axis_index(name) for name in ("half", "rest"))
    rows = min(ROWS, virt_count)

    kept = lax.dynamic_index_in_dim(cycle_panels, half, 0, keepdims=False)
    given = lax.dynamic_index_in_dim(cycle_panels, 1 - half, 0, keepdims=False)
    got = lax.ppermute(given, "half", SWAP)
    block = jnp.where(half == 0, jnp.stack([kept, got]), jnp.stack([got, kept]))[None]
    for axis, size in (("rest", n_rest), ("grp", n_grp)):
        step = size // 2
        while step:
            swapped = lax.ppermute(block, axis, [(i, i ^ step) for i in range(size)])
            low = lax.axis_index(axis) & step == 0
            block = jnp.where(low, jnp.concatenate([block, swapped]), jnp.concatenate([swapped, block]))
            step //= 2

    chunks = [(p, a) for p in range(per_dev) for a in range(0, virt_count, rows)]
    own, other = [], []
    for n, (p, a) in enumerate(chunks):
        whole, fock = amps[p], vv_fock
        if n >= DEPTH:
            whole, fock = after((whole, fock), other[n - DEPTH])
        piece = (
            jnp.dot(fock[a : a + rows], whole, preferred_element_type=jnp.float32)
            + lax.dot_general(whole[a : a + rows], fock, NT, preferred_element_type=jnp.float32)
        ).astype(jnp.bfloat16)
        own.append(piece)
        other.append(lax.ppermute(piece, "half", SWAP))

    block = after(block, other[min(len(chunks) - 1, 5)])
    bits = (n_rest * n_grp).bit_length() - 1
    panel = block.reshape(*(2,) * bits, *block.shape[1:])
    panel = panel.transpose(*range(bits)[::-1], bits, bits + 1, bits + 2)
    panel = panel.reshape(n_rest, n_grp, *block.shape[1:])
    panel = panel.transpose(2, 0, 3, 1, 4).reshape(virt_count, 2, virt_count)
    own_panel = lax.dynamic_index_in_dim(panel, half, 1, keepdims=False)
    other_panel = lax.dynamic_index_in_dim(panel, 1 - half, 1, keepdims=False)

    row = lax.dynamic_index_in_dim(row_energy, half, 0, keepdims=False)
    out = jnp.zeros(amps.shape, jnp.bfloat16)
    for (p, a), mine, theirs in zip(chunks, own, other):
        total = (
            mine.astype(jnp.float32)
            + lax.dot_general(mine, own_panel, NT, preferred_element_type=jnp.float32)
            + lax.dot_general(theirs, other_panel, NT, preferred_element_type=jnp.float32)
        )
        col = lax.dynamic_index_in_dim(col_energy, (rest * per_dev + p) % group_j, 0, keepdims=False)
        divisor = ((virt_energy[a : a + rows, None] + virt_energy[None, :]) - row) - col
        out = lax.dynamic_update_slice(out, (total / divisor).astype(jnp.bfloat16)[None], (p, a, 0))
    return out[None]


def solution(mesh):
    n_grp, n_pair = mesh.shape["grp"], mesh.shape["pair"]
    split = Mesh(mesh.devices.reshape(n_grp, 2, n_pair // 2), ("grp", "half", "rest"))
    pair = ("half", "rest")
    in_specs = (P("grp", pair, None, None), P(), P(None, pair, "grp"), P(), P("grp"), P())
    out_specs = P("grp", pair, None, None)
    return jax.shard_map(shards, mesh=split, in_specs=in_specs, out_specs=out_specs, check_vma=False)
```

```python
import jax
import jax.numpy as jnp
from jax import lax
from jax.experimental import pallas as pl
from jax.experimental.pallas import tpu as pltpu
from jax.sharding import Mesh, PartitionSpec as P

ROWS = 256
COLS = 256
DEPTH = 3
VMEM = 48 * 1024 * 1024
PANEL_STEPS = [0, 0, 1, 0, 1, 1, 1, 1, 2, 2, 1]
SWAP = [(0, 1), (1, 0)]
NT = (((1,), (1,)), ((), ()))


def dot_nt(x, y):
    return lax.dot_general(x, y, NT, preferred_element_type=jnp.float32)


def dress_kernel(f_rows, t_cols, t_rows, f_cols, *rest):
    out = rest[-1]
    total = jnp.dot(f_rows[...], t_cols[...], preferred_element_type=jnp.float32)
    out[...] = (total + dot_nt(t_rows[...], f_cols[...])).astype(out.dtype)


def dress(amplitudes, fock, pair, first_row, rows, events):
    virt = fock.shape[0]
    cols = min(COLS, virt)
    block = first_row // rows
    return pl.pallas_call(
        dress_kernel,
        out_shape=jax.ShapeDtypeStruct((rows, virt), jnp.bfloat16),
        grid=(virt // cols,),
        in_specs=[
            pl.BlockSpec((rows, virt), lambda j: (block, 0)),
            pl.BlockSpec((None, None, virt, cols), lambda j: (0, pair, 0, j)),
            pl.BlockSpec((None, None, rows, virt), lambda j: (0, pair, block, 0)),
            pl.BlockSpec((cols, virt), lambda j: (j, 0)),
        ]
        + [pl.BlockSpec(memory_space=pltpu.HBM)] * len(events),
        out_specs=pl.BlockSpec((rows, cols), lambda j: (0, j)),
        compiler_params=pltpu.CompilerParams(vmem_limit_bytes=VMEM),
        cost_estimate=pl.CostEstimate(
            flops=4 * rows * virt * virt, bytes_accessed=4 * virt * virt + 6 * rows * virt, transcendentals=0
        ),
    )(fock, amplitudes, amplitudes, fock, *events)


def finish_kernel(energies, mine, own_cols, theirs, panel_own, panel_other, a_energy, b_energy, *rest):
    out = rest[-1]
    total = dot_nt(mine[...], panel_own[...]) + dot_nt(theirs[...], panel_other[...])
    total = total + own_cols[...].astype(jnp.float32)
    divisor = ((a_energy[...] + b_energy[...]) - energies[0]) - energies[1]
    out[...] = (total / divisor).astype(out.dtype)


def finish(out, shape, pair, first_row, energies, mine, theirs, panel, a_energy, b_energy, events):
    rows, virt = mine.shape
    cols = min(COLS, virt)
    block = first_row // rows
    behind = list(events) + ([] if out is None else [out])
    return pl.pallas_call(
        finish_kernel,
        out_shape=jax.ShapeDtypeStruct(shape, jnp.bfloat16),
        grid=(virt // cols,),
        in_specs=[
            pl.BlockSpec(memory_space=pltpu.SMEM),
            pl.BlockSpec((rows, virt), lambda j: (0, 0)),
            pl.BlockSpec((rows, cols), lambda j: (0, j)),
            pl.BlockSpec((rows, virt), lambda j: (0, 0)),
            pl.BlockSpec((None, cols, virt), lambda j: (0, j, 0)),
            pl.BlockSpec((None, cols, virt), lambda j: (1, j, 0)),
            pl.BlockSpec((rows, 1), lambda j: (block, 0)),
            pl.BlockSpec((1, cols), lambda j: (0, j)),
        ]
        + [pl.BlockSpec(memory_space=pltpu.HBM)] * len(behind),
        out_specs=pl.BlockSpec((None, None, rows, cols), lambda j: (0, pair, block, j)),
        input_output_aliases={} if out is None else {7 + len(behind): 0},
        compiler_params=pltpu.CompilerParams(vmem_limit_bytes=VMEM),
        cost_estimate=pl.CostEstimate(
            flops=4 * rows * virt * virt, bytes_accessed=4 * virt * virt + 6 * rows * virt, transcendentals=0
        ),
    )(energies, mine, mine, theirs, panel, panel, a_energy, b_energy, *behind)


def join_kernel(first, block, swapped, *rest):
    out = rest[-1]
    out[first[0]] = block[...]
    out[1 - first[0]] = swapped[...]


def join_columns_kernel(first, block, swapped, *rest):
    out = rest[-1]
    cols = block.shape[2]

    @pl.when(first[0] == 0)
    def _():
        out[:, :, :cols] = block[...]
        out[:, :, cols:] = swapped[...]

    @pl.when(first[0] == 1)
    def _():
        out[:, :, :cols] = swapped[...]
        out[:, :, cols:] = block[...]


def join_kernel(place, block, swapped, *rest):
    out = rest[-1]
    out[:, place[0]] = block[...]
    out[:, 1 - place[0]] = swapped[...]


def join(block, swapped, place, events):
    lead, rows, cols = block.shape
    joined = pl.pallas_call(
        join_kernel,
        out_shape=jax.ShapeDtypeStruct((lead, 2, rows, cols), block.dtype),
        in_specs=[pl.BlockSpec(memory_space=pltpu.SMEM)]
        + [pl.BlockSpec(memory_space=pltpu.VMEM)] * 2
        + [pl.BlockSpec(memory_space=pltpu.HBM)] * len(events),
        out_specs=pl.BlockSpec(memory_space=pltpu.VMEM),
        compiler_params=pltpu.CompilerParams(vmem_limit_bytes=VMEM),
    )(place[None], block, swapped, *events)
    return joined.reshape(2 * lead, rows, cols)


def place_kernel(where, block, *rest):
    rest[-1][...] = block[...]


def place(panel, block, where, col_blocks, events):
    lead, rows, cols = block.shape
    behind = list(events) + ([] if panel is None else [panel])
    return pl.pallas_call(
        place_kernel,
        out_shape=jax.ShapeDtypeStruct((2, lead, 2, rows, col_blocks * cols), block.dtype),
        grid_spec=pltpu.PrefetchScalarGridSpec(
            num_scalar_prefetch=1,
            grid=(1,),
            in_specs=[pl.BlockSpec((lead, rows, cols), lambda i, w: (0, 0, 0))]
            + [pl.BlockSpec(memory_space=pltpu.HBM)] * len(behind),
            out_specs=pl.BlockSpec((None, lead, None, rows, cols), lambda i, w: (w[0], 0, w[1], 0, w[2])),
        ),
        input_output_aliases={} if panel is None else {1 + len(behind): 0},
        compiler_params=pltpu.CompilerParams(vmem_limit_bytes=VMEM),
    )(where, block, *behind)


def shards(amplitudes, vv_fock, cycle_panels, row_energy, col_energy, virt_energy):
    per_dev, virt_count = amplitudes.shape[1:3]
    group_j = col_energy.shape[0]
    half, rest = lax.axis_index("half"), lax.axis_index("rest")
    n_rest, n_grp = lax.axis_size("rest"), lax.axis_size("grp")
    rows = min(ROWS, virt_count)
    chunks = [(p, a) for p in range(per_dev) for a in range(0, virt_count, rows)]

    row = lax.dynamic_index_in_dim(row_energy, half, 0, keepdims=False)
    cols = lax.dynamic_slice_in_dim(col_energy, (rest * per_dev) % group_j, per_dev)
    energies = [jnp.stack([row, cols[p]]) for p in range(per_dev)]
    a_energy, b_energy = virt_energy[:, None], virt_energy[None, :]

    own, other = [], []

    def send(n, events):
        piece = dress(amplitudes, vv_fock, *chunks[n], rows, events)
        own.append(piece)
        other.append(lax.ppermute(piece, "half", SWAP))

    given = lax.dynamic_index_in_dim(cycle_panels, 1 - half, 0, keepdims=False)
    kept = lax.dynamic_index_in_dim(cycle_panels, half, 0, keepdims=False)
    got = lax.ppermute(given, "half", SWAP)
    send(0, [])
    grp, col_blocks = lax.axis_index("grp"), n_grp // 2
    steps = [1 << bit for bit in range(n_rest.bit_length() - 2, 0, -1)]
    others = [(g, r) for g in range(n_grp - 1, -1, -1) for r in (1, 0)]
    block, panel, swapped = None, None, None

    def start_swap():
        return lax.ppermute(block, "rest", [(i, i ^ steps[0]) for i in range(n_rest)]) if steps else None

    def next_panel_step(last_piece):
        nonlocal block, panel, swapped
        if block is None:
            block = join(kept[None], got[None], half, [last_piece])
            swapped = start_swap()
        elif steps:
            step = steps.pop(0)
            block = join(block, swapped, (rest & step) // step, [last_piece])
            swapped = start_swap()
        else:
            g, r = others.pop()
            part = block
            if g or r:
                pairs = [(i * n_rest + j, (i ^ g) * n_rest + (j ^ r)) for i in range(n_grp) for j in range(n_rest)]
                part = lax.ppermute(block, ("grp", "rest"), pairs)
            from_grp = grp ^ g
            where = jnp.stack([(from_grp // col_blocks) ^ half, (rest ^ r) & 1, from_grp % col_blocks])
            panel = place(panel, part, where, col_blocks, [last_piece])

    out, finished = None, 0

    def end(n, events):
        whole = panel.reshape(2, virt_count, virt_count)
        return finish(
            out, amplitudes.shape, *chunks[n], energies[chunks[n][0]], own[n], other[n], whole, a_energy, b_energy, events
        )

    for n in range(1, len(chunks)):
        events = [own[n - 1]] + [x for x in (out, panel, block) if x is not None][:1]
        if n >= DEPTH:
            events.append(other[n - DEPTH])
        send(n, events)
        for _ in range(PANEL_STEPS[n] if n < len(PANEL_STEPS) else 0):
            if others:
                next_panel_step(own[n])
        while not others and finished <= min(2 * (n - 10) + 1, n - DEPTH):
            out = end(finished, [own[n]])
            finished += 1
    while others:
        next_panel_step(own[-1])
    for n in range(finished, len(chunks)):
        out = end(n, [own[-1]])
    return out


def solution(mesh):
    n_grp, n_pair = mesh.shape["grp"], mesh.shape["pair"]
    split = Mesh(mesh.devices.reshape(n_grp, 2, n_pair // 2), ("grp", "half", "rest"))
    pair = ("half", "rest")
    in_specs = (P("grp", pair, None, None), P(), P(None, pair, "grp"), P(), P("grp"), P())
    out_specs = P("grp", pair, None, None)
    return jax.shard_map(shards, mesh=split, in_specs=in_specs, out_specs=out_specs, check_vma=False)
```

```python
import jax
import jax.numpy as jnp
from jax import lax
from jax.experimental import pallas as pl
from jax.experimental.pallas import tpu as pltpu
from jax.sharding import Mesh, PartitionSpec as P

ROWS = 256
COLS = 256
DEPTH = 3
VMEM = 48 * 1024 * 1024
LAST_VMEM = 24 * 1024 * 1024
PANEL_STEPS = [0, 0, 1, 0, 1, 1, 1, 1, 2, 2, 1]
SWAP = [(0, 1), (1, 0)]
NT = (((1,), (1,)), ((), ()))


def dot_nt(x, y):
    return lax.dot_general(x, y, NT, preferred_element_type=jnp.float32)


def dress_kernel(f_rows, t_cols, t_rows, f_cols, *rest):
    out = rest[-1]
    total = jnp.dot(f_rows[...], t_cols[...], preferred_element_type=jnp.float32)
    out[...] = (total + dot_nt(t_rows[...], f_cols[...])).astype(out.dtype)


def dress(amplitudes, fock, pair, first_row, rows, events):
    virt = fock.shape[0]
    cols = min(COLS, virt)
    block = first_row // rows
    return pl.pallas_call(
        dress_kernel,
        out_shape=jax.ShapeDtypeStruct((rows, virt), jnp.bfloat16),
        grid=(virt // cols,),
        in_specs=[
            pl.BlockSpec((rows, virt), lambda j: (block, 0)),
            pl.BlockSpec((None, None, virt, cols), lambda j: (0, pair, 0, j)),
            pl.BlockSpec((None, None, rows, virt), lambda j: (0, pair, block, 0)),
            pl.BlockSpec((cols, virt), lambda j: (j, 0)),
        ]
        + [pl.BlockSpec(memory_space=pltpu.HBM)] * len(events),
        out_specs=pl.BlockSpec((rows, cols), lambda j: (0, j)),
        compiler_params=pltpu.CompilerParams(vmem_limit_bytes=VMEM),
        cost_estimate=pl.CostEstimate(
            flops=4 * rows * virt * virt, bytes_accessed=4 * virt * virt + 6 * rows * virt, transcendentals=0
        ),
    )(fock, amplitudes, amplitudes, fock, *events)


def finish_kernel(energies, mine, own_cols, theirs, panel_own, panel_other, a_energy, b_energy, *rest):
    out = rest[-1]
    total = dot_nt(mine[...], panel_own[...]) + dot_nt(theirs[...], panel_other[...])
    total = total + own_cols[...].astype(jnp.float32)
    divisor = ((a_energy[...] + b_energy[...]) - energies[0]) - energies[1]
    out[...] = (total / divisor).astype(out.dtype)


def finish(out, shape, pair, first_row, energies, mine, theirs, panel, a_energy, b_energy, events):
    rows, virt = mine.shape
    cols = min(COLS, virt)
    block = first_row // rows
    behind = list(events) + ([] if out is None else [out])
    return pl.pallas_call(
        finish_kernel,
        out_shape=jax.ShapeDtypeStruct(shape, jnp.bfloat16),
        grid=(virt // cols,),
        in_specs=[
            pl.BlockSpec(memory_space=pltpu.SMEM),
            pl.BlockSpec((rows, virt), lambda j: (0, 0)),
            pl.BlockSpec((rows, cols), lambda j: (0, j)),
            pl.BlockSpec((rows, virt), lambda j: (0, 0)),
            pl.BlockSpec((None, cols, virt), lambda j: (0, j, 0)),
            pl.BlockSpec((None, cols, virt), lambda j: (1, j, 0)),
            pl.BlockSpec((rows, 1), lambda j: (block, 0)),
            pl.BlockSpec((1, cols), lambda j: (0, j)),
        ]
        + [pl.BlockSpec(memory_space=pltpu.HBM)] * len(behind),
        out_specs=pl.BlockSpec((None, None, rows, cols), lambda j: (0, pair, block, j)),
        input_output_aliases={} if out is None else {7 + len(behind): 0},
        compiler_params=pltpu.CompilerParams(vmem_limit_bytes=VMEM),
        cost_estimate=pl.CostEstimate(
            flops=4 * rows * virt * virt, bytes_accessed=4 * virt * virt + 6 * rows * virt, transcendentals=0
        ),
    )(energies, mine, mine, theirs, panel, panel, a_energy, b_energy, *behind)


def half_finish_kernel(mine, panel_own, panel_other, out, other_out):
    out[...] = mine[...].astype(jnp.float32) + dot_nt(mine[...], panel_own[...])
    other_out[...] = panel_other[...]


def half_finish(mine, panel):
    rows, virt = mine.shape
    return pl.pallas_call(
        half_finish_kernel,
        out_shape=(jax.ShapeDtypeStruct((rows, virt), jnp.float32), jax.ShapeDtypeStruct((virt, virt), panel.dtype)),
        grid_spec=pl.GridSpec(
            grid=(1,),
            in_specs=[
                pl.BlockSpec((rows, virt), lambda i: (0, 0)),
                pl.BlockSpec((None, virt, virt), lambda i: (0, 0, 0)),
                pl.BlockSpec((None, virt, virt), lambda i: (1, 0, 0)),
            ],
            out_specs=(pl.BlockSpec((rows, virt), lambda i: (0, 0)), pl.BlockSpec((virt, virt), lambda i: (0, 0))),
        ),
        compiler_params=pltpu.CompilerParams(vmem_limit_bytes=LAST_VMEM),
    )(mine, panel, panel)


def last_finish_kernel(energies, part, theirs, panel_other, a_energy, b_energy, _, out):
    total = part[...] + dot_nt(theirs[...], panel_other[...])
    divisor = ((a_energy[...] + b_energy[...]) - energies[0]) - energies[1]
    out[...] = (total / divisor).astype(out.dtype)


def last_finish(out, pair, first_row, energies, part, theirs, panel_other, a_energy, b_energy):
    rows, virt = theirs.shape
    block = first_row // rows
    whole = pl.BlockSpec(memory_space=pltpu.VMEM)
    return pl.pallas_call(
        last_finish_kernel,
        out_shape=jax.ShapeDtypeStruct(out.shape, out.dtype),
        grid=(1,),
        in_specs=[
            pl.BlockSpec(memory_space=pltpu.SMEM),
            whole,
            whole,
            whole,
            pl.BlockSpec((rows, 1), lambda i: (block, 0)),
            whole,
            pl.BlockSpec(memory_space=pltpu.HBM),
        ],
        out_specs=pl.BlockSpec((None, None, rows, virt), lambda i: (0, pair, block, 0)),
        input_output_aliases={6: 0},
        compiler_params=pltpu.CompilerParams(vmem_limit_bytes=LAST_VMEM),
    )(energies, part, theirs, panel_other, a_energy, b_energy, out)


def join_kernel(first, block, swapped, *rest):
    out = rest[-1]
    out[first[0]] = block[...]
    out[1 - first[0]] = swapped[...]


def join_columns_kernel(first, block, swapped, *rest):
    out = rest[-1]
    cols = block.shape[2]

    @pl.when(first[0] == 0)
    def _():
        out[:, :, :cols] = block[...]
        out[:, :, cols:] = swapped[...]

    @pl.when(first[0] == 1)
    def _():
        out[:, :, :cols] = swapped[...]
        out[:, :, cols:] = block[...]


def join_kernel(place, block, swapped, *rest):
    out = rest[-1]
    out[:, place[0]] = block[...]
    out[:, 1 - place[0]] = swapped[...]


def join(block, swapped, place, events):
    lead, rows, cols = block.shape
    joined = pl.pallas_call(
        join_kernel,
        out_shape=jax.ShapeDtypeStruct((lead, 2, rows, cols), block.dtype),
        in_specs=[pl.BlockSpec(memory_space=pltpu.SMEM)]
        + [pl.BlockSpec(memory_space=pltpu.VMEM)] * 2
        + [pl.BlockSpec(memory_space=pltpu.HBM)] * len(events),
        out_specs=pl.BlockSpec(memory_space=pltpu.VMEM),
        compiler_params=pltpu.CompilerParams(vmem_limit_bytes=VMEM),
    )(place[None], block, swapped, *events)
    return joined.reshape(2 * lead, rows, cols)


def place_kernel(where, block, *rest):
    rest[-1][...] = block[...]


def place(panel, block, where, col_blocks, events):
    lead, rows, cols = block.shape
    behind = list(events) + ([] if panel is None else [panel])
    return pl.pallas_call(
        place_kernel,
        out_shape=jax.ShapeDtypeStruct((2, lead, 2, rows, col_blocks * cols), block.dtype),
        grid_spec=pltpu.PrefetchScalarGridSpec(
            num_scalar_prefetch=1,
            grid=(1,),
            in_specs=[pl.BlockSpec((lead, rows, cols), lambda i, w: (0, 0, 0))]
            + [pl.BlockSpec(memory_space=pltpu.HBM)] * len(behind),
            out_specs=pl.BlockSpec((None, lead, None, rows, cols), lambda i, w: (w[0], 0, w[1], 0, w[2])),
        ),
        input_output_aliases={} if panel is None else {1 + len(behind): 0},
        compiler_params=pltpu.CompilerParams(vmem_limit_bytes=VMEM),
    )(where, block, *behind)


def shards(amplitudes, vv_fock, cycle_panels, row_energy, col_energy, virt_energy):
    per_dev, virt_count = amplitudes.shape[1:3]
    group_j = col_energy.shape[0]
    half, rest = lax.axis_index("half"), lax.axis_index("rest")
    n_rest, n_grp = lax.axis_size("rest"), lax.axis_size("grp")
    rows = min(ROWS, virt_count)
    chunks = [(p, a, rows) for p in range(per_dev) for a in range(0, virt_count, rows)]

    row = lax.dynamic_index_in_dim(row_energy, half, 0, keepdims=False)
    cols = lax.dynamic_slice_in_dim(col_energy, (rest * per_dev) % group_j, per_dev)
    energies = [jnp.stack([row, cols[p]]) for p in range(per_dev)]
    a_energy, b_energy = virt_energy[:, None], virt_energy[None, :]

    own, other = [], []

    def send(n, events):
        piece = dress(amplitudes, vv_fock, *chunks[n], events)
        own.append(piece)
        other.append(lax.ppermute(piece, "half", SWAP))

    given = lax.dynamic_index_in_dim(cycle_panels, 1 - half, 0, keepdims=False)
    kept = lax.dynamic_index_in_dim(cycle_panels, half, 0, keepdims=False)
    got = lax.ppermute(given, "half", SWAP)
    send(0, [])
    grp, col_blocks = lax.axis_index("grp"), n_grp // 2
    steps = [1 << bit for bit in range(n_rest.bit_length() - 2, 0, -1)]
    others = [(g, r) for g in range(n_grp - 1, -1, -1) for r in (1, 0)]
    block, panel, swapped = None, None, None

    def start_swap():
        return lax.ppermute(block, "rest", [(i, i ^ steps[0]) for i in range(n_rest)]) if steps else None

    def next_panel_step(last_piece):
        nonlocal block, panel, swapped
        if block is None:
            block = join(kept[None], got[None], half, [last_piece])
            swapped = start_swap()
        elif steps:
            step = steps.pop(0)
            block = join(block, swapped, (rest & step) // step, [last_piece])
            swapped = start_swap()
        else:
            g, r = others.pop()
            part = block
            if g or r:
                pairs = [(i * n_rest + j, (i ^ g) * n_rest + (j ^ r)) for i in range(n_grp) for j in range(n_rest)]
                part = lax.ppermute(block, ("grp", "rest"), pairs)
            from_grp = grp ^ g
            where = jnp.stack([(from_grp // col_blocks) ^ half, (rest ^ r) & 1, from_grp % col_blocks])
            panel = place(panel, part, where, col_blocks, [last_piece])

    out, finished = None, 0

    def end(n, events):
        whole = panel.reshape(2, virt_count, virt_count)
        return finish(
            out, amplitudes.shape, *chunks[n][:2], energies[chunks[n][0]], own[n], other[n], whole, a_energy, b_energy, events
        )

    for n in range(1, len(chunks)):
        events = [own[n - 1]] + [x for x in (out, panel, block) if x is not None][:1]
        if n >= DEPTH:
            events.append(other[n - DEPTH])
        send(n, events)
        for _ in range(PANEL_STEPS[n] if n < len(PANEL_STEPS) else 0):
            if others:
                next_panel_step(own[n])
        while not others and finished <= min(2 * (n - 10) + 1, n - DEPTH):
            out = end(finished, [own[n]])
            finished += 1
    while others:
        next_panel_step(own[-1])
    part, panel_other = half_finish(own[-1], panel.reshape(2, virt_count, virt_count))
    for n in range(finished, len(chunks) - 1):
        out = end(n, [own[-1]])
    p, a, _ = chunks[-1]
    out = last_finish(out, p, a, energies[p], part, other[-1], panel_other, a_energy, b_energy)
    return out


def solution(mesh):
    n_grp, n_pair = mesh.shape["grp"], mesh.shape["pair"]
    split = Mesh(mesh.devices.reshape(n_grp, 2, n_pair // 2), ("grp", "half", "rest"))
    pair = ("half", "rest")
    in_specs = (P("grp", pair, None, None), P(), P(None, pair, "grp"), P(), P("grp"), P())
    out_specs = P("grp", pair, None, None)
    return jax.shard_map(shards, mesh=split, in_specs=in_specs, out_specs=out_specs, check_vma=False)
```

```python
import jax
import jax.numpy as jnp
from jax import lax
from jax.experimental import pallas as pl
from jax.experimental.pallas import tpu as pltpu
from jax.sharding import Mesh, PartitionSpec as P

ROWS = 256
COLS = 256
DEPTH = 3
VMEM = 48 * 1024 * 1024
LAST_VMEM = 24 * 1024 * 1024
PANEL_STEPS = [0, 0, 1, 0, 1, 1, 1, 1, 2, 2, 1]
SWAP = [(0, 1), (1, 0)]
NT = (((1,), (1,)), ((), ()))


def dot_nt(x, y):
    return lax.dot_general(x, y, NT, preferred_element_type=jnp.float32)


def dress_kernel(f_rows, t_cols, t_rows, f_cols, *rest):
    out = rest[-1]
    total = jnp.dot(f_rows[...], t_cols[...], preferred_element_type=jnp.float32)
    out[...] = (total + dot_nt(t_rows[...], f_cols[...])).astype(out.dtype)


def dress(amplitudes, fock, pair, first_row, rows, events):
    virt = fock.shape[0]
    cols = min(COLS, virt) if events else virt
    block = first_row // rows
    return pl.pallas_call(
        dress_kernel,
        out_shape=jax.ShapeDtypeStruct((rows, virt), jnp.bfloat16),
        grid=(virt // cols,),
        in_specs=[
            pl.BlockSpec((rows, virt), lambda j: (block, 0)),
            pl.BlockSpec((None, None, virt, cols), lambda j: (0, pair, 0, j)),
            pl.BlockSpec((None, None, rows, virt), lambda j: (0, pair, block, 0)),
            pl.BlockSpec((cols, virt), lambda j: (j, 0)),
        ]
        + [pl.BlockSpec(memory_space=pltpu.HBM)] * len(events),
        out_specs=pl.BlockSpec((rows, cols), lambda j: (0, j)),
        compiler_params=pltpu.CompilerParams(vmem_limit_bytes=VMEM),
        cost_estimate=pl.CostEstimate(
            flops=4 * rows * virt * virt, bytes_accessed=4 * virt * virt + 6 * rows * virt, transcendentals=0
        ),
    )(fock, amplitudes, amplitudes, fock, *events)


def finish_kernel(energies, mine, own_cols, theirs, panel_own, panel_other, a_energy, b_energy, *rest):
    out = rest[-1]
    total = dot_nt(mine[...], panel_own[...]) + dot_nt(theirs[...], panel_other[...])
    total = total + own_cols[...].astype(jnp.float32)
    divisor = ((a_energy[...] + b_energy[...]) - energies[0]) - energies[1]
    out[...] = (total / divisor).astype(out.dtype)


def finish(out, shape, pair, first_row, energies, mine, theirs, panel, a_energy, b_energy, events):
    rows, virt = mine.shape
    cols = min(COLS, virt)
    block = first_row // rows
    behind = list(events) + ([] if out is None else [out])
    return pl.pallas_call(
        finish_kernel,
        out_shape=jax.ShapeDtypeStruct(shape, jnp.bfloat16),
        grid=(virt // cols,),
        in_specs=[
            pl.BlockSpec(memory_space=pltpu.SMEM),
            pl.BlockSpec((rows, virt), lambda j: (0, 0)),
            pl.BlockSpec((rows, cols), lambda j: (0, j)),
            pl.BlockSpec((rows, virt), lambda j: (0, 0)),
            pl.BlockSpec((None, cols, virt), lambda j: (0, j, 0)),
            pl.BlockSpec((None, cols, virt), lambda j: (1, j, 0)),
            pl.BlockSpec((rows, 1), lambda j: (block, 0)),
            pl.BlockSpec((1, cols), lambda j: (0, j)),
        ]
        + [pl.BlockSpec(memory_space=pltpu.HBM)] * len(behind),
        out_specs=pl.BlockSpec((None, None, rows, cols), lambda j: (0, pair, block, j)),
        input_output_aliases={} if out is None else {7 + len(behind): 0},
        compiler_params=pltpu.CompilerParams(vmem_limit_bytes=VMEM),
        cost_estimate=pl.CostEstimate(
            flops=4 * rows * virt * virt, bytes_accessed=4 * virt * virt + 6 * rows * virt, transcendentals=0
        ),
    )(energies, mine, mine, theirs, panel, panel, a_energy, b_energy, *behind)


def half_finish_kernel(mine, panel_own, panel_other, out, other_out):
    out[...] = mine[...].astype(jnp.float32) + dot_nt(mine[...], panel_own[...])
    other_out[...] = panel_other[...]


def half_finish(mine, panel):
    rows, virt = mine.shape
    return pl.pallas_call(
        half_finish_kernel,
        out_shape=(jax.ShapeDtypeStruct((rows, virt), jnp.float32), jax.ShapeDtypeStruct((virt, virt), panel.dtype)),
        grid_spec=pl.GridSpec(
            grid=(1,),
            in_specs=[
                pl.BlockSpec((rows, virt), lambda i: (0, 0)),
                pl.BlockSpec((None, virt, virt), lambda i: (0, 0, 0)),
                pl.BlockSpec((None, virt, virt), lambda i: (1, 0, 0)),
            ],
            out_specs=(pl.BlockSpec((rows, virt), lambda i: (0, 0)), pl.BlockSpec((virt, virt), lambda i: (0, 0))),
        ),
        compiler_params=pltpu.CompilerParams(vmem_limit_bytes=LAST_VMEM),
    )(mine, panel, panel)


def last_finish_kernel(energies, part, theirs, panel_other, a_energy, b_energy, _, out):
    total = part[...] + dot_nt(theirs[...], panel_other[...])
    divisor = ((a_energy[...] + b_energy[...]) - energies[0]) - energies[1]
    out[...] = (total / divisor).astype(out.dtype)


def last_finish(out, pair, first_row, energies, part, theirs, panel_other, a_energy, b_energy):
    rows, virt = theirs.shape
    block = first_row // rows
    whole = pl.BlockSpec(memory_space=pltpu.VMEM)
    return pl.pallas_call(
        last_finish_kernel,
        out_shape=jax.ShapeDtypeStruct(out.shape, out.dtype),
        grid=(1,),
        in_specs=[
            pl.BlockSpec(memory_space=pltpu.SMEM),
            whole,
            whole,
            whole,
            pl.BlockSpec((rows, 1), lambda i: (block, 0)),
            whole,
            pl.BlockSpec(memory_space=pltpu.HBM),
        ],
        out_specs=pl.BlockSpec((None, None, rows, virt), lambda i: (0, pair, block, 0)),
        input_output_aliases={6: 0},
        compiler_params=pltpu.CompilerParams(vmem_limit_bytes=LAST_VMEM),
    )(energies, part, theirs, panel_other, a_energy, b_energy, out)


def join_kernel(first, block, swapped, *rest):
    out = rest[-1]
    out[first[0]] = block[...]
    out[1 - first[0]] = swapped[...]


def join_columns_kernel(first, block, swapped, *rest):
    out = rest[-1]
    cols = block.shape[2]

    @pl.when(first[0] == 0)
    def _():
        out[:, :, :cols] = block[...]
        out[:, :, cols:] = swapped[...]

    @pl.when(first[0] == 1)
    def _():
        out[:, :, :cols] = swapped[...]
        out[:, :, cols:] = block[...]


def join_kernel(place, block, swapped, *rest):
    out = rest[-1]
    out[:, place[0]] = block[...]
    out[:, 1 - place[0]] = swapped[...]


def join(block, swapped, place, events):
    lead, rows, cols = block.shape
    joined = pl.pallas_call(
        join_kernel,
        out_shape=jax.ShapeDtypeStruct((lead, 2, rows, cols), block.dtype),
        in_specs=[pl.BlockSpec(memory_space=pltpu.SMEM)]
        + [pl.BlockSpec(memory_space=pltpu.VMEM)] * 2
        + [pl.BlockSpec(memory_space=pltpu.HBM)] * len(events),
        out_specs=pl.BlockSpec(memory_space=pltpu.VMEM),
        compiler_params=pltpu.CompilerParams(vmem_limit_bytes=VMEM),
    )(place[None], block, swapped, *events)
    return joined.reshape(2 * lead, rows, cols)


def place_kernel(where, block, *rest):
    rest[-1][...] = block[...]


def place(panel, block, where, col_blocks, events):
    lead, rows, cols = block.shape
    behind = list(events) + ([] if panel is None else [panel])
    return pl.pallas_call(
        place_kernel,
        out_shape=jax.ShapeDtypeStruct((2, lead, 2, rows, col_blocks * cols), block.dtype),
        grid_spec=pltpu.PrefetchScalarGridSpec(
            num_scalar_prefetch=1,
            grid=(1,),
            in_specs=[pl.BlockSpec((lead, rows, cols), lambda i, w: (0, 0, 0))]
            + [pl.BlockSpec(memory_space=pltpu.HBM)] * len(behind),
            out_specs=pl.BlockSpec((None, lead, None, rows, cols), lambda i, w: (w[0], 0, w[1], 0, w[2])),
        ),
        input_output_aliases={} if panel is None else {1 + len(behind): 0},
        compiler_params=pltpu.CompilerParams(vmem_limit_bytes=VMEM),
    )(where, block, *behind)


def shards(amplitudes, vv_fock, cycle_panels, row_energy, col_energy, virt_energy):
    per_dev, virt_count = amplitudes.shape[1:3]
    group_j = col_energy.shape[0]
    half, rest = lax.axis_index("half"), lax.axis_index("rest")
    n_rest, n_grp = lax.axis_size("rest"), lax.axis_size("grp")
    rows = min(ROWS, virt_count)
    chunks = [(p, a, rows) for p in range(per_dev) for a in range(0, virt_count, rows)]

    row = lax.dynamic_index_in_dim(row_energy, half, 0, keepdims=False)
    cols = lax.dynamic_slice_in_dim(col_energy, (rest * per_dev) % group_j, per_dev)
    energies = [jnp.stack([row, cols[p]]) for p in range(per_dev)]
    a_energy, b_energy = virt_energy[:, None], virt_energy[None, :]

    own, other = [], []

    def send(n, events):
        piece = dress(amplitudes, vv_fock, *chunks[n], events)
        own.append(piece)
        other.append(lax.ppermute(piece, "half", SWAP))

    given = lax.dynamic_index_in_dim(cycle_panels, 1 - half, 0, keepdims=False)
    kept = lax.dynamic_index_in_dim(cycle_panels, half, 0, keepdims=False)
    got = lax.ppermute(given, "half", SWAP)
    send(0, [])
    grp, col_blocks = lax.axis_index("grp"), n_grp // 2
    steps = [1 << bit for bit in range(n_rest.bit_length() - 2, 0, -1)]
    others = [(g, r) for g in range(n_grp - 1, -1, -1) for r in (1, 0)]
    block, panel, swapped = None, None, None

    def start_swap():
        return lax.ppermute(block, "rest", [(i, i ^ steps[0]) for i in range(n_rest)]) if steps else None

    def next_panel_step(last_piece):
        nonlocal block, panel, swapped
        if block is None:
            block = join(kept[None], got[None], half, [last_piece])
            swapped = start_swap()
        elif steps:
            step = steps.pop(0)
            block = join(block, swapped, (rest & step) // step, [last_piece])
            swapped = start_swap()
        else:
            g, r = others.pop()
            part = block
            if g or r:
                pairs = [(i * n_rest + j, (i ^ g) * n_rest + (j ^ r)) for i in range(n_grp) for j in range(n_rest)]
                part = lax.ppermute(block, ("grp", "rest"), pairs)
            from_grp = grp ^ g
            where = jnp.stack([(from_grp // col_blocks) ^ half, (rest ^ r) & 1, from_grp % col_blocks])
            panel = place(panel, part, where, col_blocks, [last_piece])

    out, finished = None, 0

    def end(n, events):
        whole = panel.reshape(2, virt_count, virt_count)
        return finish(
            out, amplitudes.shape, *chunks[n][:2], energies[chunks[n][0]], own[n], other[n], whole, a_energy, b_energy, events
        )

    for n in range(1, len(chunks)):
        events = [own[n - 1]] + [x for x in (out, panel, block) if x is not None][:1]
        if n >= DEPTH:
            events.append(other[n - DEPTH])
        send(n, events)
        for _ in range(PANEL_STEPS[n] if n < len(PANEL_STEPS) else 0):
            if others:
                next_panel_step(own[n])
        while not others and finished <= min(2 * (n - 10) + 1, n - DEPTH):
            out = end(finished, [own[n]])
            finished += 1
    while others:
        next_panel_step(own[-1])
    part, panel_other = half_finish(own[-1], panel.reshape(2, virt_count, virt_count))
    for n in range(finished, len(chunks) - 1):
        out = end(n, [own[-1]])
    p, a, _ = chunks[-1]
    out = last_finish(out, p, a, energies[p], part, other[-1], panel_other, a_energy, b_energy)
    return out


def solution(mesh):
    n_grp, n_pair = mesh.shape["grp"], mesh.shape["pair"]
    split = Mesh(mesh.devices.reshape(n_grp, 2, n_pair // 2), ("grp", "half", "rest"))
    pair = ("half", "rest")
    in_specs = (P("grp", pair, None, None), P(), P(None, pair, "grp"), P(), P("grp"), P())
    out_specs = P("grp", pair, None, None)
    return jax.shard_map(shards, mesh=split, in_specs=in_specs, out_specs=out_specs, check_vma=False)
```

```python
import jax
import jax.numpy as jnp
from jax import lax
from jax.experimental import pallas as pl
from jax.experimental.pallas import tpu as pltpu
from jax.sharding import Mesh, PartitionSpec as P

ROWS = 256
COLS = 256
DEPTH = 3
VMEM = 48 * 1024 * 1024
LAST_VMEM = 24 * 1024 * 1024
PANEL_STEPS = [0, 0, 1, 0, 1, 1, 1, 1, 2, 2, 1]
SWAP = [(0, 1), (1, 0)]
NT = (((1,), (1,)), ((), ()))


def dot_nt(x, y):
    return lax.dot_general(x, y, NT, preferred_element_type=jnp.float32)


def dress_kernel(f_rows, t_cols, t_rows, f_cols, *rest):
    out = rest[-1]
    total = jnp.dot(f_rows[...], t_cols[...], preferred_element_type=jnp.float32)
    out[...] = (total + dot_nt(t_rows[...], f_cols[...])).astype(out.dtype)


def dress(amplitudes, fock, pair, first_row, rows, events):
    virt = fock.shape[0]
    cols = min(COLS, virt) if events else virt
    block = first_row // rows
    return pl.pallas_call(
        dress_kernel,
        out_shape=jax.ShapeDtypeStruct((rows, virt), jnp.bfloat16),
        grid=(virt // cols,),
        in_specs=[
            pl.BlockSpec((rows, virt), lambda j: (block, 0)),
            pl.BlockSpec((None, None, virt, cols), lambda j: (0, pair, 0, j)),
            pl.BlockSpec((None, None, rows, virt), lambda j: (0, pair, block, 0)),
            pl.BlockSpec((cols, virt), lambda j: (j, 0)),
        ]
        + [pl.BlockSpec(memory_space=pltpu.HBM)] * len(events),
        out_specs=pl.BlockSpec((rows, cols), lambda j: (0, j)),
        compiler_params=pltpu.CompilerParams(vmem_limit_bytes=VMEM),
        cost_estimate=pl.CostEstimate(
            flops=4 * rows * virt * virt, bytes_accessed=4 * virt * virt + 6 * rows * virt, transcendentals=0
        ),
    )(fock, amplitudes, amplitudes, fock, *events)


def finish_kernel(energies, mine, own_cols, theirs, panel_own, panel_other, a_energy, b_energy, *rest):
    out = rest[-1]
    total = dot_nt(mine[...], panel_own[...]) + dot_nt(theirs[...], panel_other[...])
    total = total + own_cols[...].astype(jnp.float32)
    divisor = ((a_energy[...] + b_energy[...]) - energies[0]) - energies[1]
    out[...] = (total / divisor).astype(out.dtype)


def finish(out, shape, pair, first_row, energies, mine, theirs, panel, a_energy, b_energy, events):
    rows, virt = mine.shape
    cols = min(COLS, virt)
    block = first_row // rows
    behind = list(events) + ([] if out is None else [out])
    return pl.pallas_call(
        finish_kernel,
        out_shape=jax.ShapeDtypeStruct(shape, jnp.bfloat16),
        grid=(virt // cols,),
        in_specs=[
            pl.BlockSpec(memory_space=pltpu.SMEM),
            pl.BlockSpec((rows, virt), lambda j: (0, 0)),
            pl.BlockSpec((rows, cols), lambda j: (0, j)),
            pl.BlockSpec((rows, virt), lambda j: (0, 0)),
            pl.BlockSpec((None, cols, virt), lambda j: (0, j, 0)),
            pl.BlockSpec((None, cols, virt), lambda j: (1, j, 0)),
            pl.BlockSpec((rows, 1), lambda j: (block, 0)),
            pl.BlockSpec((1, cols), lambda j: (0, j)),
        ]
        + [pl.BlockSpec(memory_space=pltpu.HBM)] * len(behind),
        out_specs=pl.BlockSpec((None, None, rows, cols), lambda j: (0, pair, block, j)),
        input_output_aliases={} if out is None else {7 + len(behind): 0},
        compiler_params=pltpu.CompilerParams(vmem_limit_bytes=VMEM),
        cost_estimate=pl.CostEstimate(
            flops=4 * rows * virt * virt, bytes_accessed=4 * virt * virt + 6 * rows * virt, transcendentals=0
        ),
    )(energies, mine, mine, theirs, panel, panel, a_energy, b_energy, *behind)


def half_finish_kernel(energies, mine, panel_own, panel_other, a_energy, b_energy, part, divisor, other_out):
    part[...] = mine[...].astype(jnp.float32) + dot_nt(mine[...], panel_own[...])
    divisor[...] = ((a_energy[...] + b_energy[...]) - energies[0]) - energies[1]
    other_out[...] = panel_other[...]


def half_finish(energies, first_row, mine, panel, a_energy, b_energy):
    rows, virt = mine.shape
    block = first_row // rows
    full = pl.BlockSpec((rows, virt), lambda i: (0, 0))
    square = pl.BlockSpec((virt, virt), lambda i: (0, 0))
    shape = jax.ShapeDtypeStruct((rows, virt), jnp.float32)
    return pl.pallas_call(
        half_finish_kernel,
        out_shape=(shape, shape, jax.ShapeDtypeStruct((virt, virt), panel.dtype)),
        grid_spec=pl.GridSpec(
            grid=(1,),
            in_specs=[
                pl.BlockSpec(memory_space=pltpu.SMEM),
                full,
                pl.BlockSpec((None, virt, virt), lambda i: (0, 0, 0)),
                pl.BlockSpec((None, virt, virt), lambda i: (1, 0, 0)),
                pl.BlockSpec((rows, 1), lambda i: (block, 0)),
                pl.BlockSpec((1, virt), lambda i: (0, 0)),
            ],
            out_specs=(full, full, square),
        ),
        compiler_params=pltpu.CompilerParams(vmem_limit_bytes=LAST_VMEM),
    )(energies, mine, panel, panel, a_energy, b_energy)


def last_finish_kernel(part, divisor, theirs, panel_other, _, out):
    cols = out.shape[-1]
    here = pl.ds(pl.multiple_of(pl.program_id(0) * cols, cols), cols)
    total = part[:, here] + dot_nt(theirs[...], panel_other[here, :])
    out[...] = (total / divisor[:, here]).astype(out.dtype)


def last_finish(out, pair, first_row, part, divisor, theirs, panel_other):
    rows, virt = theirs.shape
    block, cols = first_row // rows, min(2 * COLS, virt)
    return pl.pallas_call(
        last_finish_kernel,
        out_shape=jax.ShapeDtypeStruct(out.shape, out.dtype),
        grid=(virt // cols,),
        in_specs=[pl.BlockSpec(memory_space=pltpu.VMEM)] * 4 + [pl.BlockSpec(memory_space=pltpu.HBM)],
        out_specs=pl.BlockSpec((None, None, rows, cols), lambda j: (0, pair, block, j)),
        input_output_aliases={4: 0},
        compiler_params=pltpu.CompilerParams(vmem_limit_bytes=LAST_VMEM),
    )(part, divisor, theirs, panel_other, out)


def join_kernel(first, block, swapped, *rest):
    out = rest[-1]
    out[first[0]] = block[...]
    out[1 - first[0]] = swapped[...]


def join_columns_kernel(first, block, swapped, *rest):
    out = rest[-1]
    cols = block.shape[2]

    @pl.when(first[0] == 0)
    def _():
        out[:, :, :cols] = block[...]
        out[:, :, cols:] = swapped[...]

    @pl.when(first[0] == 1)
    def _():
        out[:, :, :cols] = swapped[...]
        out[:, :, cols:] = block[...]


def join_kernel(place, block, swapped, *rest):
    out = rest[-1]
    out[:, place[0]] = block[...]
    out[:, 1 - place[0]] = swapped[...]


def join(block, swapped, place, events):
    lead, rows, cols = block.shape
    joined = pl.pallas_call(
        join_kernel,
        out_shape=jax.ShapeDtypeStruct((lead, 2, rows, cols), block.dtype),
        in_specs=[pl.BlockSpec(memory_space=pltpu.SMEM)]
        + [pl.BlockSpec(memory_space=pltpu.VMEM)] * 2
        + [pl.BlockSpec(memory_space=pltpu.HBM)] * len(events),
        out_specs=pl.BlockSpec(memory_space=pltpu.VMEM),
        compiler_params=pltpu.CompilerParams(vmem_limit_bytes=VMEM),
    )(place[None], block, swapped, *events)
    return joined.reshape(2 * lead, rows, cols)


def place_kernel(where, block, *rest):
    rest[-1][...] = block[...]


def place(panel, block, where, col_blocks, events):
    lead, rows, cols = block.shape
    behind = list(events) + ([] if panel is None else [panel])
    return pl.pallas_call(
        place_kernel,
        out_shape=jax.ShapeDtypeStruct((2, lead, 2, rows, col_blocks * cols), block.dtype),
        grid_spec=pltpu.PrefetchScalarGridSpec(
            num_scalar_prefetch=1,
            grid=(1,),
            in_specs=[pl.BlockSpec((lead, rows, cols), lambda i, w: (0, 0, 0))]
            + [pl.BlockSpec(memory_space=pltpu.HBM)] * len(behind),
            out_specs=pl.BlockSpec((None, lead, None, rows, cols), lambda i, w: (w[0], 0, w[1], 0, w[2])),
        ),
        input_output_aliases={} if panel is None else {1 + len(behind): 0},
        compiler_params=pltpu.CompilerParams(vmem_limit_bytes=VMEM),
    )(where, block, *behind)


def shards(amplitudes, vv_fock, cycle_panels, row_energy, col_energy, virt_energy):
    per_dev, virt_count = amplitudes.shape[1:3]
    group_j = col_energy.shape[0]
    half, rest = lax.axis_index("half"), lax.axis_index("rest")
    n_rest, n_grp = lax.axis_size("rest"), lax.axis_size("grp")
    rows = min(ROWS, virt_count)
    chunks = [(p, a, rows) for p in range(per_dev) for a in range(0, virt_count, rows)]
    p, a, size = chunks.pop()
    chunks += [(p, a, size // 2), (p, a + size // 2, size // 2)]

    row = lax.dynamic_index_in_dim(row_energy, half, 0, keepdims=False)
    cols = lax.dynamic_slice_in_dim(col_energy, (rest * per_dev) % group_j, per_dev)
    energies = [jnp.stack([row, cols[p]]) for p in range(per_dev)]
    a_energy, b_energy = virt_energy[:, None], virt_energy[None, :]

    own, other = [], []

    def send(n, events):
        piece = dress(amplitudes, vv_fock, *chunks[n], events)
        own.append(piece)
        other.append(lax.ppermute(piece, "half", SWAP))

    given = lax.dynamic_index_in_dim(cycle_panels, 1 - half, 0, keepdims=False)
    kept = lax.dynamic_index_in_dim(cycle_panels, half, 0, keepdims=False)
    got = lax.ppermute(given, "half", SWAP)
    send(0, [])
    grp, col_blocks = lax.axis_index("grp"), n_grp // 2
    steps = [1 << bit for bit in range(n_rest.bit_length() - 2, 0, -1)]
    others = [(g, r) for g in range(n_grp - 1, -1, -1) for r in (1, 0)]
    block, panel, swapped = None, None, None

    def start_swap():
        return lax.ppermute(block, "rest", [(i, i ^ steps[0]) for i in range(n_rest)]) if steps else None

    def next_panel_step(last_piece):
        nonlocal block, panel, swapped
        if block is None:
            block = join(kept[None], got[None], half, [last_piece])
            swapped = start_swap()
        elif steps:
            step = steps.pop(0)
            block = join(block, swapped, (rest & step) // step, [last_piece])
            swapped = start_swap()
        else:
            g, r = others.pop()
            part = block
            if g or r:
                pairs = [(i * n_rest + j, (i ^ g) * n_rest + (j ^ r)) for i in range(n_grp) for j in range(n_rest)]
                part = lax.ppermute(block, ("grp", "rest"), pairs)
            from_grp = grp ^ g
            where = jnp.stack([(from_grp // col_blocks) ^ half, (rest ^ r) & 1, from_grp % col_blocks])
            panel = place(panel, part, where, col_blocks, [last_piece])

    out, finished = None, 0

    def end(n, events):
        whole = panel.reshape(2, virt_count, virt_count)
        return finish(
            out, amplitudes.shape, *chunks[n][:2], energies[chunks[n][0]], own[n], other[n], whole, a_energy, b_energy, events
        )

    for n in range(1, len(chunks)):
        events = [own[n - 1]] + [x for x in (out, panel, block) if x is not None][:1]
        if n >= DEPTH:
            events.append(other[n - DEPTH])
        send(n, events)
        for _ in range(PANEL_STEPS[n] if n < len(PANEL_STEPS) else 0):
            if others:
                next_panel_step(own[n])
        while not others and finished <= min(2 * (n - 10) + 1, n - DEPTH):
            out = end(finished, [own[n]])
            finished += 1
    while others:
        next_panel_step(own[-1])
    p, a, _ = chunks[-1]
    whole = panel.reshape(2, virt_count, virt_count)
    part, divisor, panel_other = half_finish(energies[p], a, own[-1], whole, a_energy, b_energy)
    for n in range(finished, len(chunks) - 1):
        out = end(n, [own[-1]])
    out = last_finish(out, p, a, part, divisor, other[-1], panel_other)
    return out


def solution(mesh):
    n_grp, n_pair = mesh.shape["grp"], mesh.shape["pair"]
    split = Mesh(mesh.devices.reshape(n_grp, 2, n_pair // 2), ("grp", "half", "rest"))
    pair = ("half", "rest")
    in_specs = (P("grp", pair, None, None), P(), P(None, pair, "grp"), P(), P("grp"), P())
    out_specs = P("grp", pair, None, None)
    return jax.shard_map(shards, mesh=split, in_specs=in_specs, out_specs=out_specs, check_vma=False)
```

```python
import jax
import jax.numpy as jnp
from jax import lax
from jax.experimental import pallas as pl
from jax.experimental.pallas import tpu as pltpu
from jax.sharding import Mesh, PartitionSpec as P

ROWS = 256
COLS = 256
DEPTH = 3
VMEM = 48 * 1024 * 1024
LAST_VMEM = 24 * 1024 * 1024
PANEL_STEPS = [0, 0, 1, 0, 1] + [1] * 8
SWAP = [(0, 1), (1, 0)]
NT = (((1,), (1,)), ((), ()))


def dot_nt(x, y):
    return lax.dot_general(x, y, NT, preferred_element_type=jnp.float32)


def dress_kernel(f_rows, t_cols, t_rows, f_cols, *rest):
    out = rest[-1]
    total = jnp.dot(f_rows[...], t_cols[...], preferred_element_type=jnp.float32)
    out[...] = (total + dot_nt(t_rows[...], f_cols[...])).astype(out.dtype)


def dress(amplitudes, fock, pair, first_row, rows, events):
    virt = fock.shape[0]
    cols = min(COLS, virt) if events else virt
    block = first_row // rows
    return pl.pallas_call(
        dress_kernel,
        out_shape=jax.ShapeDtypeStruct((rows, virt), jnp.bfloat16),
        grid=(virt // cols,),
        in_specs=[
            pl.BlockSpec((rows, virt), lambda j: (block, 0)),
            pl.BlockSpec((None, None, virt, cols), lambda j: (0, pair, 0, j)),
            pl.BlockSpec((None, None, rows, virt), lambda j: (0, pair, block, 0)),
            pl.BlockSpec((cols, virt), lambda j: (j, 0)),
        ]
        + [pl.BlockSpec(memory_space=pltpu.HBM)] * len(events),
        out_specs=pl.BlockSpec((rows, cols), lambda j: (0, j)),
        compiler_params=pltpu.CompilerParams(vmem_limit_bytes=VMEM),
        cost_estimate=pl.CostEstimate(
            flops=4 * rows * virt * virt, bytes_accessed=4 * virt * virt + 6 * rows * virt, transcendentals=0
        ),
    )(fock, amplitudes, amplitudes, fock, *events)


def finish_kernel(energies, mine, own_cols, theirs, panel_own, panel_other, a_energy, b_energy, *rest):
    out = rest[-1]
    total = dot_nt(mine[...], panel_own[...]) + dot_nt(theirs[...], panel_other[...])
    total = total + own_cols[...].astype(jnp.float32)
    divisor = ((a_energy[...] + b_energy[...]) - energies[0]) - energies[1]
    out[...] = (total / divisor).astype(out.dtype)


def finish(out, shape, pair, first_row, energies, mine, theirs, panel, a_energy, b_energy, events):
    rows, virt = mine.shape
    cols = min(COLS, virt)
    block = first_row // rows
    behind = list(events) + ([] if out is None else [out])
    return pl.pallas_call(
        finish_kernel,
        out_shape=jax.ShapeDtypeStruct(shape, jnp.bfloat16),
        grid=(virt // cols,),
        in_specs=[
            pl.BlockSpec(memory_space=pltpu.SMEM),
            pl.BlockSpec((rows, virt), lambda j: (0, 0)),
            pl.BlockSpec((rows, cols), lambda j: (0, j)),
            pl.BlockSpec((rows, virt), lambda j: (0, 0)),
            pl.BlockSpec((None, cols, virt), lambda j: (0, j, 0)),
            pl.BlockSpec((None, cols, virt), lambda j: (1, j, 0)),
            pl.BlockSpec((rows, 1), lambda j: (block, 0)),
            pl.BlockSpec((1, cols), lambda j: (0, j)),
        ]
        + [pl.BlockSpec(memory_space=pltpu.HBM)] * len(behind),
        out_specs=pl.BlockSpec((None, None, rows, cols), lambda j: (0, pair, block, j)),
        input_output_aliases={} if out is None else {7 + len(behind): 0},
        compiler_params=pltpu.CompilerParams(vmem_limit_bytes=VMEM),
        cost_estimate=pl.CostEstimate(
            flops=4 * rows * virt * virt, bytes_accessed=4 * virt * virt + 6 * rows * virt, transcendentals=0
        ),
    )(energies, mine, mine, theirs, panel, panel, a_energy, b_energy, *behind)


def half_finish_kernel(energies, mine, panel_own, panel_other, a_energy, b_energy, part, divisor, other_out):
    part[...] = mine[...].astype(jnp.float32) + dot_nt(mine[...], panel_own[...])
    divisor[...] = ((a_energy[...] + b_energy[...]) - energies[0]) - energies[1]
    other_out[...] = panel_other[...]


def half_finish(energies, first_row, mine, panel, a_energy, b_energy):
    rows, virt = mine.shape
    block = first_row // rows
    full = pl.BlockSpec((rows, virt), lambda i: (0, 0))
    square = pl.BlockSpec((virt, virt), lambda i: (0, 0))
    shape = jax.ShapeDtypeStruct((rows, virt), jnp.float32)
    return pl.pallas_call(
        half_finish_kernel,
        out_shape=(shape, shape, jax.ShapeDtypeStruct((virt, virt), panel.dtype)),
        grid_spec=pl.GridSpec(
            grid=(1,),
            in_specs=[
                pl.BlockSpec(memory_space=pltpu.SMEM),
                full,
                pl.BlockSpec((None, virt, virt), lambda i: (0, 0, 0)),
                pl.BlockSpec((None, virt, virt), lambda i: (1, 0, 0)),
                pl.BlockSpec((rows, 1), lambda i: (block, 0)),
                pl.BlockSpec((1, virt), lambda i: (0, 0)),
            ],
            out_specs=(full, full, square),
        ),
        compiler_params=pltpu.CompilerParams(vmem_limit_bytes=LAST_VMEM),
    )(energies, mine, panel, panel, a_energy, b_energy)


def last_finish_kernel(part, divisor, theirs, panel_other, _, out):
    cols = out.shape[-1]
    here = pl.ds(pl.multiple_of(pl.program_id(0) * cols, cols), cols)
    total = part[:, here] + dot_nt(theirs[...], panel_other[here, :])
    out[...] = (total / divisor[:, here]).astype(out.dtype)


def last_finish(out, pair, first_row, part, divisor, theirs, panel_other):
    rows, virt = theirs.shape
    block, cols = first_row // rows, min(2 * COLS, virt)
    return pl.pallas_call(
        last_finish_kernel,
        out_shape=jax.ShapeDtypeStruct(out.shape, out.dtype),
        grid=(virt // cols,),
        in_specs=[pl.BlockSpec(memory_space=pltpu.VMEM)] * 4 + [pl.BlockSpec(memory_space=pltpu.HBM)],
        out_specs=pl.BlockSpec((None, None, rows, cols), lambda j: (0, pair, block, j)),
        input_output_aliases={4: 0},
        compiler_params=pltpu.CompilerParams(vmem_limit_bytes=LAST_VMEM),
    )(part, divisor, theirs, panel_other, out)


def join_kernel(first, block, swapped, *rest):
    out = rest[-1]
    out[first[0]] = block[...]
    out[1 - first[0]] = swapped[...]


def join_columns_kernel(first, block, swapped, *rest):
    out = rest[-1]
    cols = block.shape[2]

    @pl.when(first[0] == 0)
    def _():
        out[:, :, :cols] = block[...]
        out[:, :, cols:] = swapped[...]

    @pl.when(first[0] == 1)
    def _():
        out[:, :, :cols] = swapped[...]
        out[:, :, cols:] = block[...]


def join_kernel(place, block, swapped, *rest):
    out = rest[-1]
    out[:, place[0]] = block[...]
    out[:, 1 - place[0]] = swapped[...]


def join(block, swapped, place, events):
    lead, rows, cols = block.shape
    joined = pl.pallas_call(
        join_kernel,
        out_shape=jax.ShapeDtypeStruct((lead, 2, rows, cols), block.dtype),
        in_specs=[pl.BlockSpec(memory_space=pltpu.SMEM)]
        + [pl.BlockSpec(memory_space=pltpu.VMEM)] * 2
        + [pl.BlockSpec(memory_space=pltpu.HBM)] * len(events),
        out_specs=pl.BlockSpec(memory_space=pltpu.VMEM),
        compiler_params=pltpu.CompilerParams(vmem_limit_bytes=VMEM),
    )(place[None], block, swapped, *events)
    return joined.reshape(2 * lead, rows, cols)


def place_kernel(where, block, *rest):
    rest[-1][...] = block[...]


def place(panel, block, where, col_blocks, events):
    lead, rows, cols = block.shape
    behind = list(events) + ([] if panel is None else [panel])
    return pl.pallas_call(
        place_kernel,
        out_shape=jax.ShapeDtypeStruct((2, lead, 2, rows, col_blocks * cols), block.dtype),
        grid_spec=pltpu.PrefetchScalarGridSpec(
            num_scalar_prefetch=1,
            grid=(1,),
            in_specs=[pl.BlockSpec((lead, rows, cols), lambda i, w: (0, 0, 0))]
            + [pl.BlockSpec(memory_space=pltpu.HBM)] * len(behind),
            out_specs=pl.BlockSpec((None, lead, None, rows, cols), lambda i, w: (w[0], 0, w[1], 0, w[2])),
        ),
        input_output_aliases={} if panel is None else {1 + len(behind): 0},
        compiler_params=pltpu.CompilerParams(vmem_limit_bytes=VMEM),
    )(where, block, *behind)


def shards(amplitudes, vv_fock, cycle_panels, row_energy, col_energy, virt_energy):
    per_dev, virt_count = amplitudes.shape[1:3]
    group_j = col_energy.shape[0]
    half, rest = lax.axis_index("half"), lax.axis_index("rest")
    n_rest, n_grp = lax.axis_size("rest"), lax.axis_size("grp")
    rows = min(ROWS, virt_count)
    chunks = [(p, a, rows) for p in range(per_dev) for a in range(0, virt_count, rows)]
    p, a, size = chunks.pop()
    chunks += [(p, a, size // 2), (p, a + size // 2, size // 2)]

    row = lax.dynamic_index_in_dim(row_energy, half, 0, keepdims=False)
    cols = lax.dynamic_slice_in_dim(col_energy, (rest * per_dev) % group_j, per_dev)
    energies = [jnp.stack([row, cols[p]]) for p in range(per_dev)]
    a_energy, b_energy = virt_energy[:, None], virt_energy[None, :]

    own, other = [], []

    def send(n, events):
        piece = dress(amplitudes, vv_fock, *chunks[n], events)
        own.append(piece)
        other.append(lax.ppermute(piece, "half", SWAP))

    given = lax.dynamic_index_in_dim(cycle_panels, 1 - half, 0, keepdims=False)
    kept = lax.dynamic_index_in_dim(cycle_panels, half, 0, keepdims=False)
    got = lax.ppermute(given, "half", SWAP)
    send(0, [])
    grp, col_blocks = lax.axis_index("grp"), n_grp // 2
    steps = [1 << bit for bit in range(n_rest.bit_length() - 2, 0, -1)]
    others = [(g, r) for g in range(n_grp - 1, -1, -1) for r in (1, 0)]
    block, panel, swapped = None, None, None

    def start_swap():
        return lax.ppermute(block, "rest", [(i, i ^ steps[0]) for i in range(n_rest)]) if steps else None

    def next_panel_step(last_piece):
        nonlocal block, panel, swapped
        if block is None:
            block = join(kept[None], got[None], half, [last_piece])
            swapped = start_swap()
        elif steps:
            step = steps.pop(0)
            block = join(block, swapped, (rest & step) // step, [last_piece])
            swapped = start_swap()
        else:
            g, r = others.pop()
            part = block
            if g or r:
                pairs = [(i * n_rest + j, (i ^ g) * n_rest + (j ^ r)) for i in range(n_grp) for j in range(n_rest)]
                part = lax.ppermute(block, ("grp", "rest"), pairs)
            from_grp = grp ^ g
            where = jnp.stack([(from_grp // col_blocks) ^ half, (rest ^ r) & 1, from_grp % col_blocks])
            panel = place(panel, part, where, col_blocks, [last_piece])

    out, finished = None, 0

    def end(n, events):
        whole = panel.reshape(2, virt_count, virt_count)
        return finish(
            out, amplitudes.shape, *chunks[n][:2], energies[chunks[n][0]], own[n], other[n], whole, a_energy, b_energy, events
        )

    for n in range(1, len(chunks)):
        events = [own[n - 1]] + [x for x in (out, panel, block) if x is not None][:1]
        if n >= DEPTH:
            events.append(other[n - DEPTH])
        send(n, events)
        for _ in range(PANEL_STEPS[n] if n < len(PANEL_STEPS) else 0):
            if others:
                next_panel_step(own[n])
        while not others and finished <= min(3 * (n - 12) + 2, n - DEPTH):
            out = end(finished, [own[n]])
            finished += 1
    while others:
        next_panel_step(own[-1])
    p, a, _ = chunks[-1]
    whole = panel.reshape(2, virt_count, virt_count)
    part, divisor, panel_other = half_finish(energies[p], a, own[-1], whole, a_energy, b_energy)
    for n in range(finished, len(chunks) - 1):
        out = end(n, [own[-1]])
    out = last_finish(out, p, a, part, divisor, other[-1], panel_other)
    return out


def solution(mesh):
    n_grp, n_pair = mesh.shape["grp"], mesh.shape["pair"]
    split = Mesh(mesh.devices.reshape(n_grp, 2, n_pair // 2), ("grp", "half", "rest"))
    pair = ("half", "rest")
    in_specs = (P("grp", pair, None, None), P(), P(None, pair, "grp"), P(), P("grp"), P())
    out_specs = P("grp", pair, None, None)
    return jax.shard_map(shards, mesh=split, in_specs=in_specs, out_specs=out_specs, check_vma=False)
```

```python
import jax
import jax.numpy as jnp
from jax import lax
from jax.experimental import pallas as pl
from jax.experimental.pallas import tpu as pltpu
from jax.sharding import Mesh, PartitionSpec as P

ROWS = 256
COLS = 256
DEPTH = 3
VMEM = 48 * 1024 * 1024
LAST_VMEM = 24 * 1024 * 1024
PANEL_STEPS = [0, 0, 1, 0, 1] + [1] * 8
SWAP = [(0, 1), (1, 0)]
NT = (((1,), (1,)), ((), ()))


def dot_nt(x, y):
    return lax.dot_general(x, y, NT, preferred_element_type=jnp.float32)


def dress_kernel(f_rows, t_cols, t_rows, f_cols, *rest):
    out = rest[-1]
    total = jnp.dot(f_rows[...], t_cols[...], preferred_element_type=jnp.float32)
    out[...] = (total + dot_nt(t_rows[...], f_cols[...])).astype(out.dtype)


def dress(amplitudes, fock, pair, first_row, rows, events):
    virt = fock.shape[0]
    cols = virt
    block = first_row // rows
    return pl.pallas_call(
        dress_kernel,
        out_shape=jax.ShapeDtypeStruct((rows, virt), jnp.bfloat16),
        grid=(virt // cols,),
        in_specs=[
            pl.BlockSpec((rows, virt), lambda j: (block, 0)),
            pl.BlockSpec((None, None, virt, cols), lambda j: (0, pair, 0, j)),
            pl.BlockSpec((None, None, rows, virt), lambda j: (0, pair, block, 0)),
            pl.BlockSpec((cols, virt), lambda j: (j, 0)),
        ]
        + [pl.BlockSpec(memory_space=pltpu.HBM)] * len(events),
        out_specs=pl.BlockSpec((rows, cols), lambda j: (0, j)),
        compiler_params=pltpu.CompilerParams(vmem_limit_bytes=VMEM),
        cost_estimate=pl.CostEstimate(
            flops=4 * rows * virt * virt, bytes_accessed=4 * virt * virt + 6 * rows * virt, transcendentals=0
        ),
    )(fock, amplitudes, amplitudes, fock, *events)


def finish_kernel(energies, mine, own_cols, theirs, panel_own, panel_other, a_energy, b_energy, *rest):
    out = rest[-1]
    total = dot_nt(mine[...], panel_own[...]) + dot_nt(theirs[...], panel_other[...])
    total = total + own_cols[...].astype(jnp.float32)
    divisor = ((a_energy[...] + b_energy[...]) - energies[0]) - energies[1]
    out[...] = (total / divisor).astype(out.dtype)


def finish(out, shape, pair, first_row, energies, mine, theirs, panel, a_energy, b_energy, events):
    rows, virt = mine.shape
    cols = min(COLS, virt)
    block = first_row // rows
    behind = list(events) + ([] if out is None else [out])
    return pl.pallas_call(
        finish_kernel,
        out_shape=jax.ShapeDtypeStruct(shape, jnp.bfloat16),
        grid=(virt // cols,),
        in_specs=[
            pl.BlockSpec(memory_space=pltpu.SMEM),
            pl.BlockSpec((rows, virt), lambda j: (0, 0)),
            pl.BlockSpec((rows, cols), lambda j: (0, j)),
            pl.BlockSpec((rows, virt), lambda j: (0, 0)),
            pl.BlockSpec((None, cols, virt), lambda j: (0, j, 0)),
            pl.BlockSpec((None, cols, virt), lambda j: (1, j, 0)),
            pl.BlockSpec((rows, 1), lambda j: (block, 0)),
            pl.BlockSpec((1, cols), lambda j: (0, j)),
        ]
        + [pl.BlockSpec(memory_space=pltpu.HBM)] * len(behind),
        out_specs=pl.BlockSpec((None, None, rows, cols), lambda j: (0, pair, block, j)),
        input_output_aliases={} if out is None else {7 + len(behind): 0},
        compiler_params=pltpu.CompilerParams(vmem_limit_bytes=VMEM),
        cost_estimate=pl.CostEstimate(
            flops=4 * rows * virt * virt, bytes_accessed=4 * virt * virt + 6 * rows * virt, transcendentals=0
        ),
    )(energies, mine, mine, theirs, panel, panel, a_energy, b_energy, *behind)


def half_finish_kernel(energies, mine, panel_own, panel_other, a_energy, b_energy, part, divisor, other_out):
    part[...] = mine[...].astype(jnp.float32) + dot_nt(mine[...], panel_own[...])
    divisor[...] = ((a_energy[...] + b_energy[...]) - energies[0]) - energies[1]
    other_out[...] = panel_other[...]


def half_finish(energies, first_row, mine, panel, a_energy, b_energy):
    rows, virt = mine.shape
    block = first_row // rows
    full = pl.BlockSpec((rows, virt), lambda i: (0, 0))
    square = pl.BlockSpec((virt, virt), lambda i: (0, 0))
    shape = jax.ShapeDtypeStruct((rows, virt), jnp.float32)
    return pl.pallas_call(
        half_finish_kernel,
        out_shape=(shape, shape, jax.ShapeDtypeStruct((virt, virt), panel.dtype)),
        grid_spec=pl.GridSpec(
            grid=(1,),
            in_specs=[
                pl.BlockSpec(memory_space=pltpu.SMEM),
                full,
                pl.BlockSpec((None, virt, virt), lambda i: (0, 0, 0)),
                pl.BlockSpec((None, virt, virt), lambda i: (1, 0, 0)),
                pl.BlockSpec((rows, 1), lambda i: (block, 0)),
                pl.BlockSpec((1, virt), lambda i: (0, 0)),
            ],
            out_specs=(full, full, square),
        ),
        compiler_params=pltpu.CompilerParams(vmem_limit_bytes=LAST_VMEM),
    )(energies, mine, panel, panel, a_energy, b_energy)


def last_finish_kernel(part, divisor, theirs, panel_other, _, out):
    cols = out.shape[-1]
    here = pl.ds(pl.multiple_of(pl.program_id(0) * cols, cols), cols)
    total = part[:, here] + dot_nt(theirs[...], panel_other[here, :])
    out[...] = (total / divisor[:, here]).astype(out.dtype)


def last_finish(out, pair, first_row, part, divisor, theirs, panel_other):
    rows, virt = theirs.shape
    block, cols = first_row // rows, virt
    return pl.pallas_call(
        last_finish_kernel,
        out_shape=jax.ShapeDtypeStruct(out.shape, out.dtype),
        grid=(virt // cols,),
        in_specs=[pl.BlockSpec(memory_space=pltpu.VMEM)] * 4 + [pl.BlockSpec(memory_space=pltpu.HBM)],
        out_specs=pl.BlockSpec((None, None, rows, cols), lambda j: (0, pair, block, j)),
        input_output_aliases={4: 0},
        compiler_params=pltpu.CompilerParams(vmem_limit_bytes=LAST_VMEM),
    )(part, divisor, theirs, panel_other, out)


def join_kernel(first, block, swapped, *rest):
    out = rest[-1]
    out[first[0]] = block[...]
    out[1 - first[0]] = swapped[...]


def join_columns_kernel(first, block, swapped, *rest):
    out = rest[-1]
    cols = block.shape[2]

    @pl.when(first[0] == 0)
    def _():
        out[:, :, :cols] = block[...]
        out[:, :, cols:] = swapped[...]

    @pl.when(first[0] == 1)
    def _():
        out[:, :, :cols] = swapped[...]
        out[:, :, cols:] = block[...]


def join_kernel(place, block, swapped, *rest):
    out = rest[-1]
    out[:, place[0]] = block[...]
    out[:, 1 - place[0]] = swapped[...]


def join(block, swapped, place, events):
    lead, rows, cols = block.shape
    joined = pl.pallas_call(
        join_kernel,
        out_shape=jax.ShapeDtypeStruct((lead, 2, rows, cols), block.dtype),
        in_specs=[pl.BlockSpec(memory_space=pltpu.SMEM)]
        + [pl.BlockSpec(memory_space=pltpu.VMEM)] * 2
        + [pl.BlockSpec(memory_space=pltpu.HBM)] * len(events),
        out_specs=pl.BlockSpec(memory_space=pltpu.VMEM),
        compiler_params=pltpu.CompilerParams(vmem_limit_bytes=VMEM),
    )(place[None], block, swapped, *events)
    return joined.reshape(2 * lead, rows, cols)


def place_kernel(where, block, *rest):
    rest[-1][...] = block[...]


def place(panel, block, where, col_blocks, events):
    lead, rows, cols = block.shape
    behind = list(events) + ([] if panel is None else [panel])
    return pl.pallas_call(
        place_kernel,
        out_shape=jax.ShapeDtypeStruct((2, lead, 2, rows, col_blocks * cols), block.dtype),
        grid_spec=pltpu.PrefetchScalarGridSpec(
            num_scalar_prefetch=1,
            grid=(1,),
            in_specs=[pl.BlockSpec((lead, rows, cols), lambda i, w: (0, 0, 0))]
            + [pl.BlockSpec(memory_space=pltpu.HBM)] * len(behind),
            out_specs=pl.BlockSpec((None, lead, None, rows, cols), lambda i, w: (w[0], 0, w[1], 0, w[2])),
        ),
        input_output_aliases={} if panel is None else {1 + len(behind): 0},
        compiler_params=pltpu.CompilerParams(vmem_limit_bytes=VMEM),
    )(where, block, *behind)


def shards(amplitudes, vv_fock, cycle_panels, row_energy, col_energy, virt_energy):
    per_dev, virt_count = amplitudes.shape[1:3]
    group_j = col_energy.shape[0]
    half, rest = lax.axis_index("half"), lax.axis_index("rest")
    n_rest, n_grp = lax.axis_size("rest"), lax.axis_size("grp")
    rows = min(ROWS, virt_count)
    chunks = [(p, a, rows) for p in range(per_dev) for a in range(0, virt_count, rows)]
    p, a, size = chunks.pop()
    chunks += [(p, a, size // 2), (p, a + size // 2, size // 2)]

    row = lax.dynamic_index_in_dim(row_energy, half, 0, keepdims=False)
    cols = lax.dynamic_slice_in_dim(col_energy, (rest * per_dev) % group_j, per_dev)
    energies = [jnp.stack([row, cols[p]]) for p in range(per_dev)]
    a_energy, b_energy = virt_energy[:, None], virt_energy[None, :]

    own, other = [], []

    def send(n, events):
        piece = dress(amplitudes, vv_fock, *chunks[n], events)
        own.append(piece)
        other.append(lax.ppermute(piece, "half", SWAP))

    given = lax.dynamic_index_in_dim(cycle_panels, 1 - half, 0, keepdims=False)
    kept = lax.dynamic_index_in_dim(cycle_panels, half, 0, keepdims=False)
    got = lax.ppermute(given, "half", SWAP)
    send(0, [])
    grp, col_blocks = lax.axis_index("grp"), n_grp // 2
    steps = [1 << bit for bit in range(n_rest.bit_length() - 2, 0, -1)]
    others = [(g, r) for g in range(n_grp - 1, -1, -1) for r in (1, 0)]
    block, panel, swapped = None, None, None

    def start_swap():
        return lax.ppermute(block, "rest", [(i, i ^ steps[0]) for i in range(n_rest)]) if steps else None

    def next_panel_step(last_piece):
        nonlocal block, panel, swapped
        if block is None:
            block = join(kept[None], got[None], half, [last_piece])
            swapped = start_swap()
        elif steps:
            step = steps.pop(0)
            block = join(block, swapped, (rest & step) // step, [last_piece])
            swapped = start_swap()
        else:
            g, r = others.pop()
            part = block
            if g or r:
                pairs = [(i * n_rest + j, (i ^ g) * n_rest + (j ^ r)) for i in range(n_grp) for j in range(n_rest)]
                part = lax.ppermute(block, ("grp", "rest"), pairs)
            from_grp = grp ^ g
            where = jnp.stack([(from_grp // col_blocks) ^ half, (rest ^ r) & 1, from_grp % col_blocks])
            panel = place(panel, part, where, col_blocks, [last_piece])

    out, finished = None, 0

    def end(n, events):
        whole = panel.reshape(2, virt_count, virt_count)
        return finish(
            out, amplitudes.shape, *chunks[n][:2], energies[chunks[n][0]], own[n], other[n], whole, a_energy, b_energy, events
        )

    for n in range(1, len(chunks)):
        events = [own[n - 1]] + [x for x in (out, panel, block) if x is not None][:1]
        if n >= DEPTH:
            events.append(other[n - DEPTH])
        send(n, events)
        for _ in range(PANEL_STEPS[n] if n < len(PANEL_STEPS) else 0):
            if others:
                next_panel_step(own[n])
        while not others and finished <= min(3 * (n - 12) + 2, n - DEPTH):
            out = end(finished, [own[n]])
            finished += 1
    while others:
        next_panel_step(own[-1])
    p, a, _ = chunks[-1]
    whole = panel.reshape(2, virt_count, virt_count)
    part, divisor, panel_other = half_finish(energies[p], a, own[-1], whole, a_energy, b_energy)
    for n in range(finished, len(chunks) - 1):
        out = end(n, [own[-1]])
    out = last_finish(out, p, a, part, divisor, other[-1], panel_other)
    return out


def solution(mesh):
    n_grp, n_pair = mesh.shape["grp"], mesh.shape["pair"]
    split = Mesh(mesh.devices.reshape(n_grp, 2, n_pair // 2), ("grp", "half", "rest"))
    pair = ("half", "rest")
    in_specs = (P("grp", pair, None, None), P(), P(None, pair, "grp"), P(), P("grp"), P())
    out_specs = P("grp", pair, None, None)
    return jax.shard_map(shards, mesh=split, in_specs=in_specs, out_specs=out_specs, check_vma=False)
```

```python
import jax
import jax.numpy as jnp
from jax import lax
from jax.experimental import pallas as pl
from jax.experimental.pallas import tpu as pltpu
from jax.sharding import Mesh, PartitionSpec as P

ROWS = 256
COLS = 512
DEPTH = 3
VMEM = 48 * 1024 * 1024
LAST_VMEM = 24 * 1024 * 1024
PANEL_STEPS = [0, 0, 1, 0, 1] + [1] * 8
SWAP = [(0, 1), (1, 0)]
NT = (((1,), (1,)), ((), ()))


def dot_nt(x, y):
    return lax.dot_general(x, y, NT, preferred_element_type=jnp.float32)


def dress_kernel(f_rows, t_cols, t_rows, f_cols, *rest):
    out = rest[-1]
    total = jnp.dot(f_rows[...], t_cols[...], preferred_element_type=jnp.float32)
    out[...] = (total + dot_nt(t_rows[...], f_cols[...])).astype(out.dtype)


def dress(amplitudes, fock, pair, first_row, rows, events):
    virt = fock.shape[0]
    cols = virt
    block = first_row // rows
    return pl.pallas_call(
        dress_kernel,
        out_shape=jax.ShapeDtypeStruct((rows, virt), jnp.bfloat16),
        grid=(virt // cols,),
        in_specs=[
            pl.BlockSpec((rows, virt), lambda j: (block, 0)),
            pl.BlockSpec((None, None, virt, cols), lambda j: (0, pair, 0, j)),
            pl.BlockSpec((None, None, rows, virt), lambda j: (0, pair, block, 0)),
            pl.BlockSpec((cols, virt), lambda j: (j, 0)),
        ]
        + [pl.BlockSpec(memory_space=pltpu.HBM)] * len(events),
        out_specs=pl.BlockSpec((rows, cols), lambda j: (0, j)),
        compiler_params=pltpu.CompilerParams(vmem_limit_bytes=VMEM),
        cost_estimate=pl.CostEstimate(
            flops=4 * rows * virt * virt, bytes_accessed=4 * virt * virt + 6 * rows * virt, transcendentals=0
        ),
    )(fock, amplitudes, amplitudes, fock, *events)


def finish_kernel(energies, mine, own_cols, theirs, panel_own, panel_other, a_energy, b_energy, *rest):
    out = rest[-1]
    total = dot_nt(mine[...], panel_own[...]) + dot_nt(theirs[...], panel_other[...])
    total = total + own_cols[...].astype(jnp.float32)
    divisor = ((a_energy[...] + b_energy[...]) - energies[0]) - energies[1]
    out[...] = (total / divisor).astype(out.dtype)


def finish(out, shape, pair, first_row, energies, mine, theirs, panel, a_energy, b_energy, events):
    rows, virt = mine.shape
    cols = min(COLS, virt)
    block = first_row // rows
    behind = list(events) + ([] if out is None else [out])
    return pl.pallas_call(
        finish_kernel,
        out_shape=jax.ShapeDtypeStruct(shape, jnp.bfloat16),
        grid=(virt // cols,),
        in_specs=[
            pl.BlockSpec(memory_space=pltpu.SMEM),
            pl.BlockSpec((rows, virt), lambda j: (0, 0)),
            pl.BlockSpec((rows, cols), lambda j: (0, j)),
            pl.BlockSpec((rows, virt), lambda j: (0, 0)),
            pl.BlockSpec((None, cols, virt), lambda j: (0, j, 0)),
            pl.BlockSpec((None, cols, virt), lambda j: (1, j, 0)),
            pl.BlockSpec((rows, 1), lambda j: (block, 0)),
            pl.BlockSpec((1, cols), lambda j: (0, j)),
        ]
        + [pl.BlockSpec(memory_space=pltpu.HBM)] * len(behind),
        out_specs=pl.BlockSpec((None, None, rows, cols), lambda j: (0, pair, block, j)),
        input_output_aliases={} if out is None else {7 + len(behind): 0},
        compiler_params=pltpu.CompilerParams(vmem_limit_bytes=VMEM),
        cost_estimate=pl.CostEstimate(
            flops=4 * rows * virt * virt, bytes_accessed=4 * virt * virt + 6 * rows * virt, transcendentals=0
        ),
    )(energies, mine, mine, theirs, panel, panel, a_energy, b_energy, *behind)


def half_finish_kernel(energies, mine, panel_own, panel_other, a_energy, b_energy, part, divisor, other_out):
    part[...] = mine[...].astype(jnp.float32) + dot_nt(mine[...], panel_own[...])
    divisor[...] = ((a_energy[...] + b_energy[...]) - energies[0]) - energies[1]
    other_out[...] = panel_other[...]


def half_finish(energies, first_row, mine, panel, a_energy, b_energy):
    rows, virt = mine.shape
    block = first_row // rows
    full = pl.BlockSpec((rows, virt), lambda i: (0, 0))
    square = pl.BlockSpec((virt, virt), lambda i: (0, 0))
    shape = jax.ShapeDtypeStruct((rows, virt), jnp.float32)
    return pl.pallas_call(
        half_finish_kernel,
        out_shape=(shape, shape, jax.ShapeDtypeStruct((virt, virt), panel.dtype)),
        grid_spec=pl.GridSpec(
            grid=(1,),
            in_specs=[
                pl.BlockSpec(memory_space=pltpu.SMEM),
                full,
                pl.BlockSpec((None, virt, virt), lambda i: (0, 0, 0)),
                pl.BlockSpec((None, virt, virt), lambda i: (1, 0, 0)),
                pl.BlockSpec((rows, 1), lambda i: (block, 0)),
                pl.BlockSpec((1, virt), lambda i: (0, 0)),
            ],
            out_specs=(full, full, square),
        ),
        compiler_params=pltpu.CompilerParams(vmem_limit_bytes=LAST_VMEM),
    )(energies, mine, panel, panel, a_energy, b_energy)


def last_finish_kernel(part, divisor, theirs, panel_other, _, out):
    cols = out.shape[-1]
    here = pl.ds(pl.multiple_of(pl.program_id(0) * cols, cols), cols)
    total = part[:, here] + dot_nt(theirs[...], panel_other[here, :])
    out[...] = (total / divisor[:, here]).astype(out.dtype)


def last_finish(out, pair, first_row, part, divisor, theirs, panel_other):
    rows, virt = theirs.shape
    block, cols = first_row // rows, virt
    return pl.pallas_call(
        last_finish_kernel,
        out_shape=jax.ShapeDtypeStruct(out.shape, out.dtype),
        grid=(virt // cols,),
        in_specs=[pl.BlockSpec(memory_space=pltpu.VMEM)] * 4 + [pl.BlockSpec(memory_space=pltpu.HBM)],
        out_specs=pl.BlockSpec((None, None, rows, cols), lambda j: (0, pair, block, j)),
        input_output_aliases={4: 0},
        compiler_params=pltpu.CompilerParams(vmem_limit_bytes=LAST_VMEM),
    )(part, divisor, theirs, panel_other, out)


def join_kernel(first, block, swapped, *rest):
    out = rest[-1]
    out[first[0]] = block[...]
    out[1 - first[0]] = swapped[...]


def join_columns_kernel(first, block, swapped, *rest):
    out = rest[-1]
    cols = block.shape[2]

    @pl.when(first[0] == 0)
    def _():
        out[:, :, :cols] = block[...]
        out[:, :, cols:] = swapped[...]

    @pl.when(first[0] == 1)
    def _():
        out[:, :, :cols] = swapped[...]
        out[:, :, cols:] = block[...]


def join_kernel(place, block, swapped, *rest):
    out = rest[-1]
    out[:, place[0]] = block[...]
    out[:, 1 - place[0]] = swapped[...]


def join(block, swapped, place, events):
    lead, rows, cols = block.shape
    joined = pl.pallas_call(
        join_kernel,
        out_shape=jax.ShapeDtypeStruct((lead, 2, rows, cols), block.dtype),
        in_specs=[pl.BlockSpec(memory_space=pltpu.SMEM)]
        + [pl.BlockSpec(memory_space=pltpu.VMEM)] * 2
        + [pl.BlockSpec(memory_space=pltpu.HBM)] * len(events),
        out_specs=pl.BlockSpec(memory_space=pltpu.VMEM),
        compiler_params=pltpu.CompilerParams(vmem_limit_bytes=VMEM),
    )(place[None], block, swapped, *events)
    return joined.reshape(2 * lead, rows, cols)


def place_kernel(where, block, *rest):
    rest[-1][...] = block[...]


def place(panel, block, where, col_blocks, events):
    lead, rows, cols = block.shape
    behind = list(events) + ([] if panel is None else [panel])
    return pl.pallas_call(
        place_kernel,
        out_shape=jax.ShapeDtypeStruct((2, lead, 2, rows, col_blocks * cols), block.dtype),
        grid_spec=pltpu.PrefetchScalarGridSpec(
            num_scalar_prefetch=1,
            grid=(1,),
            in_specs=[pl.BlockSpec((lead, rows, cols), lambda i, w: (0, 0, 0))]
            + [pl.BlockSpec(memory_space=pltpu.HBM)] * len(behind),
            out_specs=pl.BlockSpec((None, lead, None, rows, cols), lambda i, w: (w[0], 0, w[1], 0, w[2])),
        ),
        input_output_aliases={} if panel is None else {1 + len(behind): 0},
        compiler_params=pltpu.CompilerParams(vmem_limit_bytes=VMEM),
    )(where, block, *behind)


def shards(amplitudes, vv_fock, cycle_panels, row_energy, col_energy, virt_energy):
    per_dev, virt_count = amplitudes.shape[1:3]
    group_j = col_energy.shape[0]
    half, rest = lax.axis_index("half"), lax.axis_index("rest")
    n_rest, n_grp = lax.axis_size("rest"), lax.axis_size("grp")
    rows = min(ROWS, virt_count)
    chunks = [(p, a, rows) for p in range(per_dev) for a in range(0, virt_count, rows)]
    p, a, size = chunks.pop()
    chunks += [(p, a, size // 2), (p, a + size // 2, size // 2)]

    row = lax.dynamic_index_in_dim(row_energy, half, 0, keepdims=False)
    cols = lax.dynamic_slice_in_dim(col_energy, (rest * per_dev) % group_j, per_dev)
    energies = [jnp.stack([row, cols[p]]) for p in range(per_dev)]
    a_energy, b_energy = virt_energy[:, None], virt_energy[None, :]

    own, other = [], []

    def send(n, events):
        piece = dress(amplitudes, vv_fock, *chunks[n], events)
        own.append(piece)
        other.append(lax.ppermute(piece, "half", SWAP))

    given = lax.dynamic_index_in_dim(cycle_panels, 1 - half, 0, keepdims=False)
    kept = lax.dynamic_index_in_dim(cycle_panels, half, 0, keepdims=False)
    got = lax.ppermute(given, "half", SWAP)
    send(0, [])
    grp, col_blocks = lax.axis_index("grp"), n_grp // 2
    steps = [1 << bit for bit in range(n_rest.bit_length() - 2, 0, -1)]
    others = [(g, r) for g in range(n_grp - 1, -1, -1) for r in (1, 0)]
    block, panel, swapped = None, None, None

    def start_swap():
        return lax.ppermute(block, "rest", [(i, i ^ steps[0]) for i in range(n_rest)]) if steps else None

    def next_panel_step(last_piece):
        nonlocal block, panel, swapped
        if block is None:
            block = join(kept[None], got[None], half, [last_piece])
            swapped = start_swap()
        elif steps:
            step = steps.pop(0)
            block = join(block, swapped, (rest & step) // step, [last_piece])
            swapped = start_swap()
        else:
            g, r = others.pop()
            part = block
            if g or r:
                pairs = [(i * n_rest + j, (i ^ g) * n_rest + (j ^ r)) for i in range(n_grp) for j in range(n_rest)]
                part = lax.ppermute(block, ("grp", "rest"), pairs)
            from_grp = grp ^ g
            where = jnp.stack([(from_grp // col_blocks) ^ half, (rest ^ r) & 1, from_grp % col_blocks])
            panel = place(panel, part, where, col_blocks, [last_piece])

    out, finished = None, 0

    def end(n, events):
        whole = panel.reshape(2, virt_count, virt_count)
        return finish(
            out, amplitudes.shape, *chunks[n][:2], energies[chunks[n][0]], own[n], other[n], whole, a_energy, b_energy, events
        )

    for n in range(1, len(chunks)):
        events = [own[n - 1]] + [x for x in (out, panel, block) if x is not None][:1]
        if n >= DEPTH:
            events.append(other[n - DEPTH])
        send(n, events)
        for _ in range(PANEL_STEPS[n] if n < len(PANEL_STEPS) else 0):
            if others:
                next_panel_step(own[n])
        while not others and finished <= min(3 * (n - 12) + 2, n - DEPTH):
            out = end(finished, [own[n]])
            finished += 1
    while others:
        next_panel_step(own[-1])
    p, a, _ = chunks[-1]
    whole = panel.reshape(2, virt_count, virt_count)
    part, divisor, panel_other = half_finish(energies[p], a, own[-1], whole, a_energy, b_energy)
    for n in range(finished, len(chunks) - 1):
        out = end(n, [own[-1]])
    out = last_finish(out, p, a, part, divisor, other[-1], panel_other)
    return out


def solution(mesh):
    n_grp, n_pair = mesh.shape["grp"], mesh.shape["pair"]
    split = Mesh(mesh.devices.reshape(n_grp, 2, n_pair // 2), ("grp", "half", "rest"))
    pair = ("half", "rest")
    in_specs = (P("grp", pair, None, None), P(), P(None, pair, "grp"), P(), P("grp"), P())
    out_specs = P("grp", pair, None, None)
    return jax.shard_map(shards, mesh=split, in_specs=in_specs, out_specs=out_specs, check_vma=False)
```
